256 devices in a mesh: tm: 16 (over x, y_lo, core), space: 16 (over y_hi, z).
Axes of the slice: x: 4, y: 4 (y_hi: 2, y_lo: 2; y = y_hi * 2 + y_lo), z: 8, core: 2. Of those that a mesh axis runs over, the one named last changes fastest.
Arguments:
- video: bfloat16 [16, 32, 160, 512], P('tm', 'space'), may hold values from -8 to 8
- gain_conv: float32 [512], replicated, may hold values from 0.25 to 1.75
- conv_weight: bfloat16 [3, 3, 512, 512], replicated, may hold values from -0.09375 to 0.09375
- gain_space: float32 [512], replicated, may hold values from 0.25 to 1.75
- query_weight: bfloat16 [512, 512], replicated, may hold values from -2 to 2
- key_weight: bfloat16 [512, 512], replicated, may hold values from -1 to 1
- value_weight: bfloat16 [512, 512], replicated, may hold values from -0.25 to 0.25
- out_weight: bfloat16 [512, 512], replicated, may hold values from -0.25 to 0.25
- gain_time: float32 [512], replicated, may hold values from 0.25 to 1.75
- time_query: bfloat16 [512, 512], replicated, may hold values from -2 to 2
- time_key: bfloat16 [512, 512], replicated, may hold values from -1 to 1
- time_value: bfloat16 [512, 512], replicated, may hold values from -0.25 to 0.25
- time_out: bfloat16 [512, 512], replicated, may hold values from -0.25 to 0.25
Outputs:
- decoded: bfloat16 [16, 32, 160, 512], P('tm', 'space')
The draws below stay inside these ranges and needn't reach their ends.
All inputs are finite; a program needn't handle non-finite values.
Results may differ from the reference program's by a relative error of at most 0.028.
Values may be sent and summed in bfloat16 or wider, within the bound.
A program may use at most 128 MiB of HBM per device.

```python
import math
import jax
import jax.numpy as jnp
from jax import lax

D = 512
W = 160
ROWS = 32
FRAMES = 16


def direction_signs(key):
    flips = jax.random.bernoulli(jax.random.fold_in(key, 101), 0.5, (D,))
    return jnp.where(flips, 1.0, -1.0).astype(jnp.float32)


def drawn_part(key):
    signs = direction_signs(key)
    return signs[:, None] * signs[None, :] / D


def random_part(key, fan_in):
    values = jnp.clip(jax.random.normal(key, (D, D), jnp.float32), -4.0, 4.0)
    return values * (1.0 / fan_in) ** 0.5


def draw_video(key, part):
    key = jax.random.fold_in(key, 5)
    values = jnp.clip(jax.random.normal(key, (FRAMES, ROWS, W, D), jnp.float32), -6.0, 6.0)
    return values.astype(jnp.bfloat16)


def draw_query_weight(key, part):
    shared = key
    key = jax.random.fold_in(key, 1)
    values = random_part(key, D / 9.0) + drawn_part(shared)
    return values.astype(jnp.bfloat16)


def draw_key_weight(key, part):
    shared = key
    key = jax.random.fold_in(key, 2)
    values = random_part(key, D * 1.0) + drawn_part(shared)
    return values.astype(jnp.bfloat16)


def draw_time_query(key, part):
    shared = key
    key = jax.random.fold_in(key, 3)
    values = random_part(key, D / 9.0) + drawn_part(shared)
    return values.astype(jnp.bfloat16)


def draw_time_key(key, part):
    shared = key
    key = jax.random.fold_in(key, 4)
    values = random_part(key, D * 1.0) + drawn_part(shared)
    return values.astype(jnp.bfloat16)


def bell_draw(own_key, extent, scale, reach, held_as=jnp.bfloat16):
    return jnp.clip(scale * jax.random.normal(own_key, extent, jnp.float32), -reach, reach).astype(held_as)


def setup_inputs(seed: int = 0) -> dict:
    streams_of = jax.random.split(jax.random.key(seed), 14)
    return {
        "video": draw_video(jax.random.fold_in(streams_of[13], 71), 0),
        "gain_conv": jnp.clip(1.0 + 0.15 * jax.random.normal(streams_of[1], (D,), jnp.float32), 0.25, 1.75),
        "conv_weight": bell_draw(streams_of[2], (3, 3, D, D), (9 * D) ** -0.5, 0.09375),
        "gain_space": jnp.clip(1.0 + 0.15 * jax.random.normal(streams_of[3], (D,), jnp.float32), 0.25, 1.75),
        "query_weight": draw_query_weight(jax.random.fold_in(streams_of[13], 71), 0),
        "key_weight": draw_key_weight(jax.random.fold_in(streams_of[13], 71), 0),
        "value_weight": bell_draw(streams_of[6], (D, D), D ** -0.5, 0.25),
        "out_weight": bell_draw(streams_of[7], (D, D), D ** -0.5, 0.25),
        "gain_time": jnp.clip(1.0 + 0.15 * jax.random.normal(streams_of[8], (D,), jnp.float32), 0.25, 1.75),
        "time_query": draw_time_query(jax.random.fold_in(streams_of[13], 71), 0),
        "time_key": draw_time_key(jax.random.fold_in(streams_of[13], 71), 0),
        "time_value": bell_draw(streams_of[11], (D, D), D ** -0.5, 0.25),
        "time_out": bell_draw(streams_of[12], (D, D), D ** -0.5, 0.25),
    }


epsilon = 1e-06

def channel_norm(inputs, gains):
    values = inputs.astype(jnp.float32)
    average = lax.optimization_barrier(jnp.mean(values, axis=-1, keepdims=True))
    centered = values - average
    spread = lax.optimization_barrier(jnp.mean(centered * centered, axis=-1, keepdims=True))
    return centered * lax.rsqrt(spread + epsilon) * gains.astype(jnp.float32)

def frame_block(frame, gain_conv, conv_weight, gain_space, query_weight, key_weight, value_weight, out_weight):
    activated = jax.nn.silu(channel_norm(frame, gain_conv)).astype(jnp.bfloat16)
    padded = jnp.pad(activated, ((1, 1), (1, 1), (0, 0)))
    convolved = jnp.zeros((ROWS * W, D), jnp.float32)
    for tap_row in range(3):
        for tap_col in range(3):
            window = padded[tap_row:tap_row + ROWS, tap_col:tap_col + W].reshape(ROWS * W, D)
            convolved = convolved + jnp.dot(window, conv_weight[tap_row, tap_col], preferred_element_type=jnp.float32)
    after_conv = (frame.reshape(ROWS * W, D).astype(jnp.float32) + convolved).astype(jnp.bfloat16)
    normed = channel_norm(after_conv, gain_space).astype(jnp.bfloat16)
    query = jnp.dot(normed, query_weight, preferred_element_type=jnp.float32).astype(jnp.bfloat16)
    key_rows = jnp.dot(normed, key_weight, preferred_element_type=jnp.float32).astype(jnp.bfloat16)
    value_rows = jnp.dot(normed, value_weight, preferred_element_type=jnp.float32).astype(jnp.bfloat16)
    scores = jnp.dot(query, key_rows.T, preferred_element_type=jnp.float32) * (1.0 / math.sqrt(D))
    highest = lax.optimization_barrier(jnp.max(scores, axis=1, keepdims=True))
    expd = jnp.exp(scores - highest)
    totals = lax.optimization_barrier(jnp.sum(expd, axis=1, keepdims=True))
    mixed = (jnp.dot(expd.astype(jnp.bfloat16), value_rows, preferred_element_type=jnp.float32) / totals).astype(jnp.bfloat16)
    after_space = (after_conv.astype(jnp.float32) + jnp.dot(mixed, out_weight, preferred_element_type=jnp.float32)).astype(jnp.bfloat16)
    return after_space

def reference(video, gain_conv, conv_weight, gain_space, query_weight, key_weight, value_weight, out_weight, gain_time, time_query, time_key, time_value, time_out):
    after_space = lax.map(lambda frame: frame_block(frame, gain_conv, conv_weight, gain_space, query_weight, key_weight, value_weight, out_weight), video)
    flat = after_space.reshape(FRAMES * ROWS * W, D)
    normed = channel_norm(flat, gain_time).astype(jnp.bfloat16)
    query = jnp.dot(normed, time_query, preferred_element_type=jnp.float32).astype(jnp.bfloat16).reshape(FRAMES, ROWS * W, D)
    key_rows = jnp.dot(normed, time_key, preferred_element_type=jnp.float32).astype(jnp.bfloat16).reshape(FRAMES, ROWS * W, D)
    value_rows = jnp.dot(normed, time_value, preferred_element_type=jnp.float32).astype(jnp.bfloat16).reshape(FRAMES, ROWS * W, D)
    scores = jnp.einsum('fnc,gnc->nfg', query.astype(jnp.float32), key_rows.astype(jnp.float32)) * (1.0 / math.sqrt(D))
    later = jnp.arange(FRAMES, dtype=jnp.int32)[:, None] >= jnp.arange(FRAMES, dtype=jnp.int32)[None, :]
    scores = jnp.where(later[None], scores, jnp.float32(-1e+30))
    highest = lax.optimization_barrier(jnp.max(scores, axis=2, keepdims=True))
    expd = jnp.exp(scores - highest)
    totals = lax.optimization_barrier(jnp.sum(expd, axis=2))
    mixed = jnp.einsum('nfg,gnc->fnc', expd.astype(jnp.bfloat16).astype(jnp.float32), value_rows.astype(jnp.float32))
    mixed = (mixed / jnp.transpose(totals)[:, :, None]).astype(jnp.bfloat16)
    decoded = flat.astype(jnp.float32) + jnp.dot(mixed.reshape(FRAMES * ROWS * W, D), time_out, preferred_element_type=jnp.float32)
    return decoded.astype(jnp.bfloat16).reshape(FRAMES, ROWS, W, D)
```

```python
import math

import jax
import jax.numpy as jnp
from jax import lax
from jax.experimental import pallas as pl
from jax.experimental.pallas import tpu as pltpu
from jax.sharding import PartitionSpec as P

epsilon = 1e-06
MESH = pl.DeviceIdType.MESH
XS, YL, CORES, YH, ZS = 4, 2, 2, 2, 8
TM = XS * YL * CORES
FRAMES = 16
W = 160
D = 512
T = 2 * W
HALF = T // 2
PIECE = 16
PIECES = T // PIECE
SCALE = 1.0 / math.sqrt(D)
LOG2E = math.log2(math.e)
BF = jnp.bfloat16
F32 = jnp.float32

ORDER = [(0, 0, 0)]
for ring, dist in [(0, 1), (1, 0), (0, 2), (1, 1), (0, 3), (1, 2), (0, 4), (1, 3), (1, 4)]:
    ORDER += [(ring, dist, 0)] if dist in (0, 4) else [(ring, dist, 0), (ring, dist, 1)]


def channel_norm(values, gains):
    average = jnp.mean(values, axis=-1, keepdims=True)
    centered = values - average
    spread = jnp.mean(centered * centered, axis=-1, keepdims=True)
    return centered * lax.rsqrt(spread + epsilon) * gains


def dot(a, b):
    return jnp.dot(a, b, preferred_element_type=F32)


def dot_t(a, b):
    return lax.dot_general(a, b, (((1,), (1,)), ((), ())), preferred_element_type=F32)


def second_owner(i):
    return i * 4 + (i % 2) * 2


def pick(t, values):
    out = jnp.int32(values[0])
    for k, v in enumerate(values):
        if k:
            out = jnp.where(t == k, jnp.int32(v), out)
    return out


def kernel(
    video, gain_conv, conv_w, gain_space, wq, wk, wv, wo, gain_time, tq, tk, tv, to,
    out,
    vid, halo, gc, gs, gt, cw, wq_v, wk_v, wv_v, wo_v, tq_v, tk_v, tv_v, to_v,
    act3, conv_acc, ac_mine, ac_t, nall, q_v, m_v, l_v, acc_v, as_t, tbuf, dbuf,
    load_sem, halo_send, halo_recv, swap_send, swap_recv,
    ring_send, sib_send, recv,
    a_send, a_recv, a_self, d_send, d_recv, d_self,
):
    tm = lax.axis_index("tm")
    sp = lax.axis_index("space")
    c = lax.rem(tm, 2)
    col = tm // 2
    h = sp // ZS
    z = lax.rem(sp, ZS)
    zp = lax.rem(z + 1, ZS)
    zm = lax.rem(z + ZS - 1, ZS)
    sibling = (col * 2 + 1 - c, sp)
    z_ids = ((tm, h * ZS + zp), (tm, h * ZS + zm))
    stays = c == h

    loads = []
    for i, (src, dst) in enumerate(
        [
            (video, vid), (gain_conv, gc), (conv_w.at[1], cw.at[1]), (conv_w.at[0], cw.at[0]),
            (conv_w.at[2], cw.at[2]), (gain_space, gs), (wq, wq_v), (wk, wk_v), (wv, wv_v), (wo, wo_v),
            (gain_time, gt), (tq, tq_v), (tk, tk_v), (tv, tv_v), (to, to_v),
        ]
    ):
        loads.append(pltpu.make_async_copy(src, dst, load_sem.at[i]))
        loads[-1].start()

    barrier = pltpu.get_barrier_semaphore()

    def greet(i, carry):
        other_tm = i // 2
        other_sp = lax.rem(i, 2) * ZS + z

        @pl.when(jnp.logical_or(other_tm != tm, other_sp != sp))
        def _():
            pl.semaphore_signal(barrier, inc=1, device_id=(other_tm, other_sp), device_id_type=MESH)

        return carry

    lax.fori_loop(0, TM * YH, greet, 0)
    for target in z_ids:
        pl.semaphore_signal(barrier, inc=1, device_id=target, device_id_type=MESH)
    crosses_down = sp == ZS - 1
    crosses_up = sp == ZS

    @pl.when(crosses_down)
    def _():
        pl.semaphore_signal(barrier, inc=1, device_id=(tm, ZS), device_id_type=MESH)

    @pl.when(crosses_up)
    def _():
        pl.semaphore_signal(barrier, inc=1, device_id=(tm, ZS - 1), device_id_type=MESH)

    crosses = jnp.where(jnp.logical_or(crosses_down, crosses_up), 1, 0)
    pl.semaphore_wait(barrier, TM * YH - 1 + 2 + crosses)

    has_up = sp > 0
    has_down = sp < YH * ZS - 1
    to_down = pltpu.make_async_remote_copy(
        src_ref=video.at[pl.ds(W, W)], dst_ref=halo.at[0], send_sem=halo_send.at[0], recv_sem=halo_recv.at[0],
        device_id=(tm, jnp.minimum(sp + 1, YH * ZS - 1)), device_id_type=MESH,
    )
    to_up = pltpu.make_async_remote_copy(
        src_ref=video.at[pl.ds(0, W)], dst_ref=halo.at[1], send_sem=halo_send.at[1], recv_sem=halo_recv.at[1],
        device_id=(tm, jnp.maximum(sp - 1, 0)), device_id_type=MESH,
    )

    @pl.when(has_down)
    def _():
        to_down.start()

    @pl.when(has_up)
    def _():
        to_up.start()

    loads[0].wait()
    loads[1].wait()
    col_index = lax.broadcasted_iota(jnp.int32, (W, D), 0)

    def activate(row, raw):
        u = channel_norm(raw.astype(F32), gc[...])
        u = (u / (1.0 + jnp.exp(-u))).astype(BF).astype(F32)
        left = jnp.where(col_index == 0, 0.0, pltpu.roll(u, 1, 0))
        right = jnp.where(col_index == W - 1, 0.0, pltpu.roll(u, W - 1, 0))
        act3[pl.ds(row * W, W), 0:D] = left.astype(BF)
        act3[pl.ds(row * W, W), D : 2 * D] = u.astype(BF)
        act3[pl.ds(row * W, W), 2 * D : 3 * D] = right.astype(BF)

    activate(1, vid[0:W])
    activate(2, vid[W:T])
    loads[2].wait()
    conv_acc[...] = vid[...].astype(F32) + dot(act3[W : 3 * W], cw[1])
    loads[3].wait()
    conv_acc[W:T] += dot(act3[W : 2 * W], cw[0])
    loads[4].wait()
    conv_acc[0:W] += dot(act3[2 * W : 3 * W], cw[2])

    @pl.when(has_up)
    def _():
        to_down.wait_recv()
        activate(0, halo[0])
        conv_acc[0:W] += dot(act3[0:W], cw[0])

    @pl.when(has_down)
    def _():
        to_up.wait_recv()
        activate(3, halo[1])
        conv_acc[W:T] += dot(act3[3 * W : 4 * W], cw[2])

    loads[5].wait()
    loads[6].wait()
    loads[7].wait()
    swap = pltpu.make_async_remote_copy(
        src_ref=ac_mine, dst_ref=ac_t, send_sem=swap_send, recv_sem=swap_recv,
        device_id=(col * 2 + 1 - c, (1 - h) * ZS + z), device_id_type=MESH,
    )

    @pl.when(stays)
    def _():
        ac_t[...] = conv_acc[...].astype(BF)

    @pl.when(jnp.logical_not(stays))
    def _():
        ac_mine[...] = conv_acc[...].astype(BF)
        swap.start()
        swap.wait_recv()

    nall[c, z] = channel_norm(ac_t[...].astype(F32), gs[...]).astype(BF)

    def origin(side, dist):
        return lax.rem(z + (ZS - dist if side == 0 else dist), ZS)

    def ring_piece(side, dist, part):
        ref = nall.at[c, origin(side, dist), pl.ds(part * HALF, HALF)]
        return pltpu.make_async_remote_copy(
            src_ref=ref, dst_ref=ref, send_sem=ring_send.at[side, dist, part], recv_sem=recv.at[c, side, dist + 1, part],
            device_id=z_ids[side], device_id_type=MESH,
        )

    def sib_piece(ring_core, side, dist, part):
        ref = nall.at[ring_core, origin(side, dist), pl.ds(part * HALF, HALF)]
        return pltpu.make_async_remote_copy(
            src_ref=ref, dst_ref=ref, send_sem=sib_send.at[side, dist, part], recv_sem=recv.at[ring_core, side, dist, part],
            device_id=sibling, device_id_type=MESH,
        )

    for part in range(2):
        for side in range(2):
            ring_piece(side, 0, part if side == 0 else 1 - part).start()
    for part in range(2):
        sib_piece(c, 0, 0, part).start()

    query = dot(nall[c, z], wq_v[...]).astype(BF)
    q_v[...] = (dot_t(query, wk_v[...]) * (SCALE * LOG2E)).astype(BF)
    m_v[...] = jnp.full(m_v.shape, -1e30, F32)
    l_v[...] = jnp.zeros(l_v.shape, F32)
    acc_v[...] = jnp.zeros(acc_v.shape, F32)

    def pieces(dist):
        if dist == 0:
            return [(0, 0), (0, 1)]
        if dist == ZS // 2:
            return [(0, 0), (1, 1)]
        return [(0, 0), (1, 1), (0, 1), (1, 0)]

    def arrive(ring, dist):
        ring_core = h if ring == 0 else 1 - h
        mine = ring_core == c
        for side, part in pieces(dist):
            wait = sib_piece(ring_core, side, dist, part)
            if dist == 0:
                @pl.when(jnp.logical_not(mine))
                def _():
                    wait.wait_recv()
                continue
            wait.wait_recv()

            @pl.when(mine)
            def _():
                if dist < ZS // 2 - 1 or (dist == ZS // 2 - 1 and side == part):
                    ring_piece(side, dist, part).start()
                sib_piece(c, side, dist, part).start()

    def attend(t, carry):
        for k, (ring, dist, side) in enumerate(ORDER):
            if side == 0:
                @pl.when(t == k)
                def _():
                    arrive(ring, dist)
        ring_t = pick(t, [r for r, _, _ in ORDER])
        off_t = pick(t, [(ZS - dist) % ZS if side == 0 else dist for _, dist, side in ORDER])
        ring_core = jnp.where(ring_t == 0, h, 1 - h)
        keys = nall[ring_core, lax.rem(z + off_t, ZS)]
        s = dot_t(q_v[...], keys)
        m_old = m_v[:, 0:1]
        m_new = jnp.maximum(m_old, jnp.max(s, axis=1, keepdims=True))
        p = jnp.exp2(s - m_new)
        alpha = jnp.exp2(m_old - m_new)
        l_v[...] = jnp.broadcast_to(l_v[:, 0:1] * alpha + jnp.sum(p, axis=1, keepdims=True), l_v.shape)
        m_v[...] = jnp.broadcast_to(m_new, m_v.shape)
        acc_v[...] = acc_v[...] * alpha + dot(p.astype(BF), keys)
        return carry

    lax.fori_loop(0, len(ORDER), attend, 0)

    loads[8].wait()
    loads[9].wait()
    mixed = (acc_v[...] / l_v[:, 0:1]).astype(BF)
    mixed = dot(mixed, wv_v[...]).astype(BF)
    as_t[...] = (ac_t[...].astype(F32) + dot(mixed, wo_v[...])).astype(BF)

    frame = col * 2 + h
    home = c * ZS + z

    def owner(j):
        i = j - TM
        return jnp.where(j < TM, j, i * 4 + lax.rem(i, 2) * 2)

    def a_piece(j, f):
        slot = j // TM
        return pltpu.make_async_remote_copy(
            src_ref=as_t.at[pl.ds(pl.multiple_of(j * PIECE, PIECE), PIECE)],
            dst_ref=tbuf.at[slot, pl.ds(pl.multiple_of(f * PIECE, PIECE), PIECE)],
            send_sem=a_send.at[j], recv_sem=a_recv.at[slot, f],
            device_id=(owner(j), home), device_id_type=MESH,
        )

    def a_local(j):
        slot = j // TM
        return pltpu.make_async_copy(
            as_t.at[pl.ds(pl.multiple_of(j * PIECE, PIECE), PIECE)],
            tbuf.at[slot, pl.ds(pl.multiple_of(frame * PIECE, PIECE), PIECE)],
            a_self.at[slot],
        )

    def is_me(j):
        return jnp.logical_and(stays, owner(j) == tm)

    def a_start(j, carry):
        @pl.when(is_me(j))
        def _():
            a_local(j).start()

        @pl.when(jnp.logical_not(is_me(j)))
        def _():
            a_piece(j, frame).start()

        return carry

    lax.fori_loop(0, PIECES, a_start, 0)
    second = tm // 4
    has_second = tm == second * 4 + lax.rem(second, 2) * 2
    for i in range(10, 15):
        loads[i].wait()

    rows = FRAMES * PIECE
    r_index = lax.broadcasted_iota(jnp.int32, (rows, rows), 0)
    c_index = lax.broadcasted_iota(jnp.int32, (rows, rows), 1)
    allowed = jnp.logical_and((r_index & (PIECE - 1)) == (c_index & (PIECE - 1)), r_index >= c_index)

    def d_piece(slot, j, f):
        return pltpu.make_async_remote_copy(
            src_ref=dbuf.at[slot, pl.ds(pl.multiple_of(f * PIECE, PIECE), PIECE)],
            dst_ref=out.at[pl.ds(pl.multiple_of(j * PIECE, PIECE), PIECE)],
            send_sem=d_send.at[slot, f], recv_sem=d_recv.at[j],
            device_id=(f, sp), device_id_type=MESH,
        )

    def d_local(slot, j):
        return pltpu.make_async_copy(
            dbuf.at[slot, pl.ds(pl.multiple_of(tm * PIECE, PIECE), PIECE)],
            out.at[pl.ds(pl.multiple_of(j * PIECE, PIECE), PIECE)],
            d_self.at[slot],
        )

    def temporal(slot, j):
        def wait_piece(f, carry):
            own = jnp.logical_and(stays, f == frame)

            @pl.when(own)
            def _():
                a_local(j).wait()

            @pl.when(jnp.logical_not(own))
            def _():
                a_piece(slot * TM, f).wait_recv()

            return carry

        lax.fori_loop(0, FRAMES, wait_piece, 0)
        x = tbuf[slot]
        normed = channel_norm(x.astype(F32), gt[...]).astype(BF)
        q = dot(normed, tq_v[...]).astype(BF)
        k = dot(normed, tk_v[...]).astype(BF)
        v = dot(normed, tv_v[...]).astype(BF)
        s = jnp.where(allowed, dot_t(q, k) * (SCALE * LOG2E), -1e30)
        p = jnp.exp2(s - jnp.max(s, axis=1, keepdims=True))
        total = jnp.sum(p, axis=1, keepdims=True)
        mix = (dot(p.astype(BF), v) / total).astype(BF)
        dbuf[slot] = (x.astype(F32) + dot(mix, to_v[...])).astype(BF)

        def d_start(f, carry):
            @pl.when(f == tm)
            def _():
                d_local(slot, j).start()

            @pl.when(f != tm)
            def _():
                d_piece(slot, j, f).start()

            return carry

        lax.fori_loop(0, FRAMES, d_start, 0)

    temporal(0, tm)

    @pl.when(has_second)
    def _():
        temporal(1, TM + second)

    def d_wait(j, carry):
        mine = owner(j) == tm

        @pl.when(mine)
        def _():
            d_local(j // TM, j).wait()

        @pl.when(jnp.logical_not(mine))
        def _():
            d_piece(0, j, tm).wait_recv()

        return carry

    lax.fori_loop(0, PIECES, d_wait, 0)

    def a_sent(j, carry):
        @pl.when(jnp.logical_not(is_me(j)))
        def _():
            a_piece(j, frame).wait_send()

        return carry

    lax.fori_loop(0, PIECES, a_sent, 0)

    def d_sent(f, carry):
        @pl.when(f != tm)
        def _():
            d_piece(0, tm, f).wait_send()

            @pl.when(has_second)
            def _():
                d_piece(1, tm, f).wait_send()

        return carry

    lax.fori_loop(0, FRAMES, d_sent, 0)

    @pl.when(has_down)
    def _():
        to_down.wait_send()

    @pl.when(has_up)
    def _():
        to_up.wait_send()

    @pl.when(jnp.logical_not(stays))
    def _():
        swap.wait_send()

    for dist in range(ZS // 2 + 1):
        for side, part in pieces(dist):
            sib_piece(c, side, dist, part).wait_send()
    for dist in range(ZS // 2):
        for side in range(2):
            for part in range(2):
                if dist < ZS // 2 - 1 or side == part:
                    ring_piece(side, dist, part).wait_send()


def local(
    video, gain_conv, conv_weight, gain_space, query_weight, key_weight, value_weight, out_weight,
    gain_time, time_query, time_key, time_value, time_out,
):
    vm = pltpu.VMEM
    dma = pltpu.SemaphoreType.DMA
    decoded = pl.pallas_call(
        kernel,
        out_shape=jax.ShapeDtypeStruct((T, D), BF),
        in_specs=[pl.BlockSpec(memory_space=pl.ANY)] * 13,
        out_specs=pl.BlockSpec(memory_space=pl.ANY),
        scratch_shapes=[
            vm((T, D), BF), vm((2, W, D), BF), vm((1, D), F32), vm((1, D), F32), vm((1, D), F32),
            vm((3, 3 * D, D), BF), *[vm((D, D), BF) for _ in range(8)],
            vm((4 * W, 3 * D), BF), vm((T, D), F32), vm((T, D), BF), vm((T, D), BF), vm((2, ZS, T, D), BF),
            vm((T, D), BF), vm((T, 128), F32), vm((T, 128), F32), vm((T, D), F32), vm((T, D), BF),
            vm((2, FRAMES * PIECE, D), BF), vm((2, FRAMES * PIECE, D), BF),
            dma((15,)), dma((2,)), dma((2,)), dma, dma,
            dma((2, 4, 2)), dma((2, 5, 2)), dma((2, 2, 5, 2)),
            dma((PIECES,)), dma((2, FRAMES)), dma((2,)), dma((2, FRAMES)), dma((PIECES,)), dma((2,)),
        ],
        compiler_params=pltpu.CompilerParams(
            collective_id=0, has_side_effects=True, vmem_limit_bytes=56 * 1024 * 1024
        ),
    )(
        video.reshape(T, D), gain_conv.reshape(1, D), conv_weight.reshape(3, 3 * D, D), gain_space.reshape(1, D),
        query_weight, key_weight, value_weight, out_weight, gain_time.reshape(1, D),
        time_query, time_key, time_value, time_out,
    )
    return decoded.reshape(1, 2, W, D)


def solution(mesh):
    return jax.shard_map(
        local,
        mesh=mesh,
        in_specs=(P("tm", "space", None, None),) + (P(),) * 12,
        out_specs=P("tm", "space", None, None),
        check_vma=False,
    )
```

```python
import math

import jax
import jax.numpy as jnp
from jax import lax
from jax.experimental import pallas as pl
from jax.experimental.pallas import tpu as pltpu
from jax.sharding import PartitionSpec as P

epsilon = 1e-06
MESH = pl.DeviceIdType.MESH
XS, YL, CORES, YH, ZS = 4, 2, 2, 2, 8
TM = XS * YL * CORES
FRAMES = 16
W = 160
D = 512
T = 2 * W
HALF = T // 2
PIECE = 16
PIECES = T // PIECE
SCALE = 1.0 / math.sqrt(D)
LOG2E = math.log2(math.e)
BF = jnp.bfloat16
F32 = jnp.float32

QUARTER = T // 4
KEYS = 2 * T
STEPS = ZS * 2 * T // KEYS


def channel_norm(values, gains):
    average = jnp.mean(values, axis=-1, keepdims=True)
    centered = values - average
    spread = jnp.mean(centered * centered, axis=-1, keepdims=True)
    return centered * lax.rsqrt(spread + epsilon) * gains


def dot(a, b):
    return jnp.dot(a, b, preferred_element_type=F32)


def dot_t(a, b):
    return lax.dot_general(a, b, (((1,), (1,)), ((), ())), preferred_element_type=F32)


def second_owner(i):
    return i * 4 + (i % 2) * 2


def kernel(
    video, gain_conv, conv_w, gain_space, wq, wk, wv, wo, gain_time, tq, tk, tv, to,
    out,
    vid, halo, gc, gs, gt, cw, wq_v, wk_v, wv_v, wo_v, tq_v, tk_v, tv_v, to_v,
    act3, conv_acc, ac_t, nall, q_v, m_v, l_v, acc_v, as_t, tbuf, dbuf,
    load_sem, halo_send, halo_recv, swap_send, swap_recv,
    ring_send, ring_recv, sib_send, sib_recv,
    a_send, a_recv, a_self, d_send, d_recv, d_self,
):
    tm = lax.axis_index("tm")
    sp = lax.axis_index("space")
    c = lax.rem(tm, 2)
    col = tm // 2
    h = sp // ZS
    z = lax.rem(sp, ZS)
    zp = lax.rem(z + 1, ZS)
    zm = lax.rem(z + ZS - 1, ZS)
    sibling = (col * 2 + 1 - c, sp)
    z_ids = ((tm, h * ZS + zp), (tm, h * ZS + zm))
    stays = c == h
    block = c * ZS + z
    last = YH * ZS - 1

    loads = []
    for i, (src, dst) in enumerate(
        [
            (gain_conv, gc), (conv_w.at[1], cw.at[1]), (conv_w.at[0], cw.at[0]),
            (conv_w.at[2], cw.at[2]), (gain_space, gs), (wq, wq_v), (wk, wk_v), (wv, wv_v), (wo, wo_v),
            (gain_time, gt), (tq, tq_v), (tk, tk_v), (tv, tv_v), (to, to_v),
        ]
    ):
        loads.append(pltpu.make_async_copy(src, dst, load_sem.at[i]))
        loads[-1].start()

    own_load = pltpu.make_async_copy(video, vid, load_sem.at[14])

    @pl.when(stays)
    def _():
        own_load.start()

    barrier = pltpu.get_barrier_semaphore()

    def greet(i, carry):
        other_tm = i // 2
        other_sp = lax.rem(i, 2) * ZS + z

        @pl.when(jnp.logical_or(other_tm != tm, other_sp != sp))
        def _():
            pl.semaphore_signal(barrier, inc=1, device_id=(other_tm, other_sp), device_id_type=MESH)

        return carry

    lax.fori_loop(0, TM * YH, greet, 0)

    def greet_z(i, carry):
        for other_z in (zp, zm):
            other = (col * 2 + lax.rem(i, 2), (i // 2) * ZS + other_z)
            pl.semaphore_signal(barrier, inc=1, device_id=other, device_id_type=MESH)
        return carry

    lax.fori_loop(0, CORES * YH, greet_z, 0)
    pl.semaphore_wait(barrier, TM * YH - 1 + 2 * CORES * YH)

    def place(s):
        return (col * 2 + lax.div(s, ZS), c * ZS + lax.rem(s, ZS))

    sends_down = sp < last
    sends_up = sp > 0
    gets_down = block > 0
    gets_up = block < last
    to_down = pltpu.make_async_remote_copy(
        src_ref=video.at[pl.ds(W, W)], dst_ref=halo.at[0], send_sem=halo_send.at[0], recv_sem=halo_recv.at[0],
        device_id=place(jnp.minimum(sp + 1, last)), device_id_type=MESH,
    )
    to_up = pltpu.make_async_remote_copy(
        src_ref=video.at[pl.ds(0, W)], dst_ref=halo.at[1], send_sem=halo_send.at[1], recv_sem=halo_recv.at[1],
        device_id=place(jnp.maximum(sp - 1, 0)), device_id_type=MESH,
    )
    swap = pltpu.make_async_remote_copy(
        src_ref=video, dst_ref=vid, send_sem=swap_send, recv_sem=swap_recv,
        device_id=place(sp), device_id_type=MESH,
    )

    away = jnp.logical_not(stays)

    @pl.when(away)
    def _():
        swap.start()

    @pl.when(sends_down)
    def _():
        to_down.start()

    @pl.when(sends_up)
    def _():
        to_up.start()

    @pl.when(stays)
    def _():
        own_load.wait()

    @pl.when(away)
    def _():
        swap.wait_recv()

    loads[0].wait()
    col_index = lax.broadcasted_iota(jnp.int32, (W, D), 0)

    def activate(row, raw):
        u = channel_norm(raw.astype(F32), gc[...])
        u = (u / (1.0 + jnp.exp(-u))).astype(BF).astype(F32)
        left = jnp.where(col_index == 0, 0.0, pltpu.roll(u, 1, 0))
        right = jnp.where(col_index == W - 1, 0.0, pltpu.roll(u, W - 1, 0))
        act3[pl.ds(row * W, W), 0:D] = left.astype(BF)
        act3[pl.ds(row * W, W), D : 2 * D] = u.astype(BF)
        act3[pl.ds(row * W, W), 2 * D : 3 * D] = right.astype(BF)

    activate(1, vid[0:W])
    activate(2, vid[W:T])
    loads[1].wait()
    conv_acc[...] = vid[...].astype(F32) + dot(act3[W : 3 * W], cw[1])
    loads[2].wait()
    conv_acc[W:T] += dot(act3[W : 2 * W], cw[0])
    loads[3].wait()
    conv_acc[0:W] += dot(act3[2 * W : 3 * W], cw[2])

    @pl.when(gets_down)
    def _():
        to_down.wait_recv()
        activate(0, halo[0])
        conv_acc[0:W] += dot(act3[0:W], cw[0])

    @pl.when(gets_up)
    def _():
        to_up.wait_recv()
        activate(3, halo[1])
        conv_acc[W:T] += dot(act3[3 * W : 4 * W], cw[2])

    loads[4].wait()
    after_conv = conv_acc[...].astype(BF)
    ac_t[...] = after_conv

    my_ring = jnp.where(stays, 0, 1)

    def place_of(ring, side, dist):
        if dist == 0:
            return ring * T
        if dist == ZS // 2:
            return (4 * dist - 2 + ring) * T
        return (4 * dist - 2 + 2 * ring + side) * T

    def rows_of(ring, side, dist, start, size):
        return nall.at[pl.ds(pl.multiple_of(place_of(ring, side, dist) + start, PIECE), size)]

    nall[pl.ds(pl.multiple_of(my_ring * T, T), T)] = channel_norm(after_conv.astype(F32), gs[...]).astype(BF)

    def ring_piece(side, dist, part):
        return pltpu.make_async_remote_copy(
            src_ref=rows_of(my_ring, side, dist, part * QUARTER, QUARTER),
            dst_ref=rows_of(my_ring, side, dist + 1, part * QUARTER, QUARTER),
            send_sem=ring_send.at[side, dist, part], recv_sem=ring_recv.at[side, dist, part],
            device_id=z_ids[side], device_id_type=MESH,
        )

    def sib_piece(ring, side, dist, half):
        ref = rows_of(ring, side, dist, half * HALF, HALF)
        return pltpu.make_async_remote_copy(
            src_ref=ref, dst_ref=ref, send_sem=sib_send.at[side, dist, half], recv_sem=sib_recv.at[side, dist, half],
            device_id=sibling, device_id_type=MESH,
        )

    parts = ((0, 1, 2, 3), (2, 3, 0, 1))

    def travels(side, dist, part):
        return dist < ZS // 2 - 1 or (dist == ZS // 2 - 1 and part // 2 == side)

    def halves(side, dist):
        if dist == 0:
            return (0, 1) if side == 0 else ()
        return (side, 1 - side) if dist < ZS // 2 else (side,)

    for i in range(4):
        for side in range(2):
            ring_piece(side, 0, parts[side][i]).start()
    for half in range(2):
        sib_piece(my_ring, 0, 0, half).start()

    loads[5].wait()
    query = dot(nall[pl.ds(pl.multiple_of(my_ring * T, T), T)], wq_v[...]).astype(BF)
    loads[6].wait()
    q_v[...] = (dot_t(query, wk_v[...]) * (SCALE * LOG2E)).astype(BF)
    m_v[...] = jnp.full(m_v.shape, -1e30, F32)
    l_v[...] = jnp.zeros(l_v.shape, F32)
    acc_v[...] = jnp.zeros(acc_v.shape, F32)

    def own(dist, half):
        if dist == ZS // 2 and half == 1:
            return
        for i in (2 * half, 2 * half + 1):
            for side in range(2):
                part = parts[side][i]
                ring_piece(side, dist - 1, part).wait_recv()
                if travels(side, dist, part):
                    ring_piece(side, dist, part).start()
        for side in range(2):
            sib_piece(my_ring, side, dist, halves(side, dist)[half]).start()

    def other(dist):
        for side in range(2):
            for half in halves(side, dist):
                sib_piece(1 - my_ring, side, dist, half).wait_recv()

    def first_ring(t):
        if t == 0:
            own(1, 0)
            other(0)
        elif t % 2 == 1:
            own((t + 1) // 2, 1)
            if t == STEPS - 1:
                other(ZS // 2)
        else:
            own(t // 2 + 1, 0)
            other(t // 2)

    def second_ring(t):
        if t == 0:
            other(0)
        elif t % 2 == 1:
            own((t + 1) // 2, 0)
            other((t + 1) // 2)
        else:
            own(t // 2, 1)

    def attend(t, carry):
        for k in range(STEPS):
            @pl.when(jnp.logical_and(t == k, stays))
            def _():
                first_ring(k)

            @pl.when(jnp.logical_and(t == k, away))
            def _():
                second_ring(k)

        keys = nall[pl.ds(pl.multiple_of(t * KEYS, KEYS), KEYS)]
        s = dot_t(q_v[...], keys)
        m_old = m_v[:, 0:1]
        m_new = jnp.maximum(m_old, jnp.max(s, axis=1, keepdims=True))
        p = jnp.exp2(s - m_new)
        alpha = jnp.exp2(m_old - m_new)
        l_v[...] = jnp.broadcast_to(l_v[:, 0:1] * alpha + jnp.sum(p, axis=1, keepdims=True), l_v.shape)
        m_v[...] = jnp.broadcast_to(m_new, m_v.shape)
        acc_v[...] = acc_v[...] * alpha + dot(p.astype(BF), keys)
        return carry

    lax.fori_loop(0, STEPS, attend, 0)

    loads[7].wait()
    loads[8].wait()
    mixed = (acc_v[...] / l_v[:, 0:1]).astype(BF)
    mixed = dot(mixed, wv_v[...]).astype(BF)
    as_t[...] = (ac_t[...].astype(F32) + dot(mixed, wo_v[...])).astype(BF)

    frame = col * 2 + h
    home = c * ZS + z

    def owner(j):
        i = j - TM
        return jnp.where(j < TM, j, i * 4 + lax.rem(i, 2) * 2)

    def a_piece(j, f):
        slot = j // TM
        return pltpu.make_async_remote_copy(
            src_ref=as_t.at[pl.ds(pl.multiple_of(j * PIECE, PIECE), PIECE)],
            dst_ref=tbuf.at[slot, pl.ds(pl.multiple_of(f * PIECE, PIECE), PIECE)],
            send_sem=a_send.at[j], recv_sem=a_recv.at[slot, f],
            device_id=(owner(j), home), device_id_type=MESH,
        )

    def a_local(j):
        slot = j // TM
        return pltpu.make_async_copy(
            as_t.at[pl.ds(pl.multiple_of(j * PIECE, PIECE), PIECE)],
            tbuf.at[slot, pl.ds(pl.multiple_of(frame * PIECE, PIECE), PIECE)],
            a_self.at[slot],
        )

    def is_me(j):
        return jnp.logical_and(stays, owner(j) == tm)

    def a_start(j, carry):
        @pl.when(is_me(j))
        def _():
            a_local(j).start()

        @pl.when(jnp.logical_not(is_me(j)))
        def _():
            a_piece(j, frame).start()

        return carry

    lax.fori_loop(0, PIECES, a_start, 0)
    second = tm // 4
    has_second = tm == second * 4 + lax.rem(second, 2) * 2
    for i in range(9, 14):
        loads[i].wait()

    rows = FRAMES * PIECE
    r_index = lax.broadcasted_iota(jnp.int32, (rows, rows), 0)
    c_index = lax.broadcasted_iota(jnp.int32, (rows, rows), 1)
    allowed = jnp.logical_and((r_index & (PIECE - 1)) == (c_index & (PIECE - 1)), r_index >= c_index)

    def d_piece(slot, j, f):
        return pltpu.make_async_remote_copy(
            src_ref=dbuf.at[slot, pl.ds(pl.multiple_of(f * PIECE, PIECE), PIECE)],
            dst_ref=out.at[pl.ds(pl.multiple_of(j * PIECE, PIECE), PIECE)],
            send_sem=d_send.at[slot, f], recv_sem=d_recv.at[j],
            device_id=(f, sp), device_id_type=MESH,
        )

    def d_local(slot, j):
        return pltpu.make_async_copy(
            dbuf.at[slot, pl.ds(pl.multiple_of(tm * PIECE, PIECE), PIECE)],
            out.at[pl.ds(pl.multiple_of(j * PIECE, PIECE), PIECE)],
            d_self.at[slot],
        )

    def temporal(slot, j):
        def wait_piece(f, carry):
            own = jnp.logical_and(stays, f == frame)

            @pl.when(own)
            def _():
                a_local(j).wait()

            @pl.when(jnp.logical_not(own))
            def _():
                a_piece(slot * TM, f).wait_recv()

            return carry

        lax.fori_loop(0, FRAMES, wait_piece, 0)
        x = tbuf[slot]
        normed = channel_norm(x.astype(F32), gt[...]).astype(BF)
        q = dot(normed, tq_v[...]).astype(BF)
        k = dot(normed, tk_v[...]).astype(BF)
        v = dot(normed, tv_v[...]).astype(BF)
        s = jnp.where(allowed, dot_t(q, k) * (SCALE * LOG2E), -1e30)
        p = jnp.exp2(s - jnp.max(s, axis=1, keepdims=True))
        total = jnp.sum(p, axis=1, keepdims=True)
        mix = (dot(p.astype(BF), v) / total).astype(BF)
        dbuf[slot] = (x.astype(F32) + dot(mix, to_v[...])).astype(BF)

        def d_start(f, carry):
            @pl.when(f == tm)
            def _():
                d_local(slot, j).start()

            @pl.when(f != tm)
            def _():
                d_piece(slot, j, f).start()

            return carry

        lax.fori_loop(0, FRAMES, d_start, 0)

    temporal(0, tm)

    @pl.when(has_second)
    def _():
        temporal(1, TM + second)

    def d_wait(j, carry):
        mine = owner(j) == tm

        @pl.when(mine)
        def _():
            d_local(j // TM, j).wait()

        @pl.when(jnp.logical_not(mine))
        def _():
            d_piece(0, j, tm).wait_recv()

        return carry

    lax.fori_loop(0, PIECES, d_wait, 0)

    def a_sent(j, carry):
        @pl.when(jnp.logical_not(is_me(j)))
        def _():
            a_piece(j, frame).wait_send()

        return carry

    lax.fori_loop(0, PIECES, a_sent, 0)

    def d_sent(f, carry):
        @pl.when(f != tm)
        def _():
            d_piece(0, tm, f).wait_send()

            @pl.when(has_second)
            def _():
                d_piece(1, tm, f).wait_send()

        return carry

    lax.fori_loop(0, FRAMES, d_sent, 0)

    @pl.when(sends_down)
    def _():
        to_down.wait_send()

    @pl.when(sends_up)
    def _():
        to_up.wait_send()

    @pl.when(away)
    def _():
        swap.wait_send()

    for dist in range(ZS // 2 + 1):
        for side in range(2):
            for half in halves(side, dist):
                sib_piece(my_ring, side, dist, half).wait_send()
            for part in parts[side]:
                if travels(side, dist, part):
                    ring_piece(side, dist, part).wait_send()


def local(
    video, gain_conv, conv_weight, gain_space, query_weight, key_weight, value_weight, out_weight,
    gain_time, time_query, time_key, time_value, time_out,
):
    vm = pltpu.VMEM
    dma = pltpu.SemaphoreType.DMA
    decoded = pl.pallas_call(
        kernel,
        out_shape=jax.ShapeDtypeStruct((T, D), BF),
        in_specs=[pl.BlockSpec(memory_space=pl.ANY)] * 13,
        out_specs=pl.BlockSpec(memory_space=pl.ANY),
        scratch_shapes=[
            vm((T, D), BF), vm((2, W, D), BF), vm((1, D), F32), vm((1, D), F32), vm((1, D), F32),
            vm((3, 3 * D, D), BF), *[vm((D, D), BF) for _ in range(8)],
            vm((4 * W, 3 * D), BF), vm((T, D), F32), vm((T, D), BF), vm((2 * ZS * T, D), BF),
            vm((T, D), BF), vm((T, 128), F32), vm((T, 128), F32), vm((T, D), F32), vm((T, D), BF),
            vm((2, FRAMES * PIECE, D), BF), vm((2, FRAMES * PIECE, D), BF),
            dma((15,)), dma((2,)), dma((2,)), dma, dma,
            dma((2, 4, 4)), dma((2, 4, 4)), dma((2, 5, 2)), dma((2, 5, 2)),
            dma((PIECES,)), dma((2, FRAMES)), dma((2,)), dma((2, FRAMES)), dma((PIECES,)), dma((2,)),
        ],
        compiler_params=pltpu.CompilerParams(
            collective_id=0, has_side_effects=True, vmem_limit_bytes=56 * 1024 * 1024
        ),
    )(
        video.reshape(T, D), gain_conv.reshape(1, D), conv_weight.reshape(3, 3 * D, D), gain_space.reshape(1, D),
        query_weight, key_weight, value_weight, out_weight, gain_time.reshape(1, D),
        time_query, time_key, time_value, time_out,
    )
    return decoded.reshape(1, 2, W, D)


def solution(mesh):
    return jax.shard_map(
        local,
        mesh=mesh,
        in_specs=(P("tm", "space", None, None),) + (P(),) * 12,
        out_specs=P("tm", "space", None, None),
        check_vma=False,
    )
```

```python
import functools
import math

import jax
import jax.numpy as jnp
from jax import lax
from jax.experimental import pallas as pl
from jax.experimental.pallas import tpu as pltpu
from jax.sharding import PartitionSpec as P

epsilon = 1e-06
MESH = pl.DeviceIdType.MESH
XS, YL, CORES, YH, ZS = 4, 2, 2, 2, 8
TM = XS * YL * CORES
FRAMES = 16
W = 160
D = 512
T = 2 * W
HALF = T // 2
PIECE = 16
PIECES = T // PIECE
SCALE = 1.0 / math.sqrt(D)
LOG2E = math.log2(math.e)
BF = jnp.bfloat16
F32 = jnp.float32

QUARTER = T // 4
KEYS = 2 * T
STEPS = ZS * 2 * T // KEYS


def channel_norm(values, gains):
    average = jnp.mean(values, axis=-1, keepdims=True)
    centered = values - average
    spread = jnp.mean(centered * centered, axis=-1, keepdims=True)
    return centered * lax.rsqrt(spread + epsilon) * gains


def dot(a, b):
    return jnp.dot(a, b, preferred_element_type=F32)


def dot_t(a, b):
    return lax.dot_general(a, b, (((1,), (1,)), ((), ())), preferred_element_type=F32)


def owner(j):
    return lax.rem(5 * j, TM)


def kernel(
    video, gain_conv, conv_w, gain_space, wq, wk, wv, wo, gain_time, tq, tk, tv, to,
    out,
    vid, halo, gc, gs, gt, cw, wq_v, wk_v, wv_v, wo_v, tq_v, tk_v, tv_v, to_v, wvo, tw,
    act3, conv_acc, ac_t, nall, q_v, m_v, l_v, acc_v, as_t, tbuf, dbuf,
    load_sem, halo_send, halo_recv, swap_send, swap_recv,
    ring_send, ring_recv, sib_send, sib_recv,
    a_send, a_recv, a_self, d_send, d_recv, d_self,
):
    tm = lax.axis_index("tm")
    sp = lax.axis_index("space")
    c = lax.rem(tm, 2)
    col = tm // 2
    h = sp // ZS
    z = lax.rem(sp, ZS)
    zp = lax.rem(z + 1, ZS)
    zm = lax.rem(z + ZS - 1, ZS)
    sibling = (col * 2 + 1 - c, sp)
    z_ids = ((tm, h * ZS + zp), (tm, h * ZS + zm))
    stays = c == h
    block = c * ZS + z
    last = YH * ZS - 1

    loads = []
    for i, (src, dst) in enumerate(
        [
            (gain_conv, gc), (conv_w.at[1], cw.at[1]), (conv_w.at[0], cw.at[0]),
            (conv_w.at[2], cw.at[2]), (gain_space, gs), (wq, wq_v), (wk, wk_v), (wv, wv_v), (wo, wo_v),
            (gain_time, gt), (tq, tq_v), (tk, tk_v), (tv, tv_v), (to, to_v),
        ]
    ):
        loads.append(pltpu.make_async_copy(src, dst, load_sem.at[i]))
        loads[-1].start()

    own_load = pltpu.make_async_copy(video, vid, load_sem.at[14])

    @pl.when(stays)
    def _():
        own_load.start()

    barrier = pltpu.get_barrier_semaphore()

    def greet(i, carry):
        other_tm = i // 2
        other_sp = lax.rem(i, 2) * ZS + z

        @pl.when(jnp.logical_or(other_tm != tm, other_sp != sp))
        def _():
            pl.semaphore_signal(barrier, inc=1, device_id=(other_tm, other_sp), device_id_type=MESH)

        return carry

    lax.fori_loop(0, TM * YH, greet, 0)

    def greet_z(i, carry):
        for other_z in (zp, zm):
            other = (col * 2 + lax.rem(i, 2), (i // 2) * ZS + other_z)
            pl.semaphore_signal(barrier, inc=1, device_id=other, device_id_type=MESH)
        return carry

    lax.fori_loop(0, CORES * YH, greet_z, 0)
    pl.semaphore_wait(barrier, TM * YH - 1 + 2 * CORES * YH)

    def place(s):
        return (col * 2 + lax.div(s, ZS), c * ZS + lax.rem(s, ZS))

    sends_down = sp < last
    sends_up = sp > 0
    gets_down = block > 0
    gets_up = block < last
    to_down = pltpu.make_async_remote_copy(
        src_ref=video.at[pl.ds(W, W)], dst_ref=halo.at[0], send_sem=halo_send.at[0], recv_sem=halo_recv.at[0],
        device_id=place(jnp.minimum(sp + 1, last)), device_id_type=MESH,
    )
    to_up = pltpu.make_async_remote_copy(
        src_ref=video.at[pl.ds(0, W)], dst_ref=halo.at[1], send_sem=halo_send.at[1], recv_sem=halo_recv.at[1],
        device_id=place(jnp.maximum(sp - 1, 0)), device_id_type=MESH,
    )
    swap = pltpu.make_async_remote_copy(
        src_ref=video, dst_ref=vid, send_sem=swap_send, recv_sem=swap_recv,
        device_id=place(sp), device_id_type=MESH,
    )

    away = jnp.logical_not(stays)

    @pl.when(away)
    def _():
        swap.start()

    @pl.when(sends_down)
    def _():
        to_down.start()

    @pl.when(sends_up)
    def _():
        to_up.start()

    @pl.when(stays)
    def _():
        own_load.wait()

    @pl.when(away)
    def _():
        swap.wait_recv()

    loads[0].wait()
    col_index = lax.broadcasted_iota(jnp.int32, (W, D), 0)

    def activate(row, raw):
        u = channel_norm(raw.astype(F32), gc[...])
        u = (u / (1.0 + jnp.exp(-u))).astype(BF).astype(F32)
        left = jnp.where(col_index == 0, 0.0, pltpu.roll(u, 1, 0))
        right = jnp.where(col_index == W - 1, 0.0, pltpu.roll(u, W - 1, 0))
        act3[pl.ds(row * W, W), 0:D] = left.astype(BF)
        act3[pl.ds(row * W, W), D : 2 * D] = u.astype(BF)
        act3[pl.ds(row * W, W), 2 * D : 3 * D] = right.astype(BF)

    activate(1, vid[0:W])
    activate(2, vid[W:T])
    loads[1].wait()
    conv_acc[...] = vid[...].astype(F32) + dot(act3[W : 3 * W], cw[1])
    loads[2].wait()
    conv_acc[W:T] += dot(act3[W : 2 * W], cw[0])
    loads[3].wait()
    conv_acc[0:W] += dot(act3[2 * W : 3 * W], cw[2])

    my_ring = jnp.where(stays, 0, 1)

    def place_of(ring, side, dist):
        if dist == 0:
            return ring * T
        if dist == ZS // 2:
            return (4 * dist - 2 + ring) * T
        return (4 * dist - 2 + 2 * ring + side) * T

    def rows_of(ring, side, dist, start, size):
        return nall.at[pl.ds(pl.multiple_of(place_of(ring, side, dist) + start, PIECE), size)]

    def ring_piece(side, dist, part):
        return pltpu.make_async_remote_copy(
            src_ref=rows_of(my_ring, side, dist, part * QUARTER, QUARTER),
            dst_ref=rows_of(my_ring, side, dist + 1, part * QUARTER, QUARTER),
            send_sem=ring_send.at[side, dist, part], recv_sem=ring_recv.at[side, dist, part],
            device_id=z_ids[side], device_id_type=MESH,
        )

    def sib_piece(ring, side, dist, half):
        ref = rows_of(ring, side, dist, half * HALF, HALF)
        return pltpu.make_async_remote_copy(
            src_ref=ref, dst_ref=ref, send_sem=sib_send.at[side, dist, half], recv_sem=sib_recv.at[side, dist, half],
            device_id=sibling, device_id_type=MESH,
        )

    parts = ((0, 1, 2, 3), (2, 3, 0, 1))

    def travels(side, dist, part):
        return dist < ZS // 2 - 1 or (dist == ZS // 2 - 1 and part // 2 == side)

    def halves(side, dist):
        if dist == 0:
            return (0, 1) if side == 0 else ()
        return (side, 1 - side) if dist < ZS // 2 else (side,)

    def finish_row(row, arrives, copy, tap):
        part = slice(row * W, (row + 1) * W)

        @pl.when(arrives)
        def _():
            copy.wait_recv()
            activate(3 * row, halo[row])
            conv_acc[part] += dot(act3[3 * row * W : (3 * row + 1) * W], cw[tap])

        after_conv = conv_acc[part].astype(BF)
        ac_t[part] = after_conv
        at = pl.multiple_of(my_ring * T + row * W, PIECE)
        nall[pl.ds(at, W)] = channel_norm(after_conv.astype(F32), gs[...]).astype(BF)
        for quarter in (2 * row, 2 * row + 1):
            for side in range(2):
                ring_piece(side, 0, quarter).start()
        sib_piece(my_ring, 0, 0, row).start()

    loads[4].wait()
    finish_row(0, gets_down, to_down, 0)
    finish_row(1, gets_up, to_up, 2)

    loads[5].wait()
    query = dot(nall[pl.ds(pl.multiple_of(my_ring * T, T), T)], wq_v[...]).astype(BF)
    loads[6].wait()
    q_v[...] = (dot_t(query, wk_v[...]) * (SCALE * LOG2E)).astype(BF)
    for i in range(7, 14):
        loads[i].wait()
    wvo[...] = dot(wv_v[...], wo_v[...]).astype(BF)
    tw[:, 0:D] = (dot_t(tq_v[...], tk_v[...]) * (SCALE * LOG2E)).astype(BF)
    tw[:, D : 2 * D] = dot(tv_v[...], to_v[...]).astype(BF)
    m_v[...] = jnp.full(m_v.shape, -1e30, F32)
    l_v[...] = jnp.zeros(l_v.shape, F32)
    acc_v[...] = jnp.zeros(acc_v.shape, F32)

    def own(dist, half):
        if dist == ZS // 2 and half == 1:
            return
        for i in (2 * half, 2 * half + 1):
            for side in range(2):
                part = parts[side][i]
                ring_piece(side, dist - 1, part).wait_recv()
                if travels(side, dist, part):
                    ring_piece(side, dist, part).start()
        for side in range(2):
            sib_piece(my_ring, side, dist, halves(side, dist)[half]).start()

    def other(dist):
        for side in range(2):
            for half in halves(side, dist):
                sib_piece(1 - my_ring, side, dist, half).wait_recv()

    order_0 = (1, 0, 3, 2, 5, 4, 6, 7)
    order_1 = (0, 1, 2, 3, 4, 5, 6, 7)
    before_0 = (
        lambda: (own(1, 0), own(1, 1)),
        lambda: (own(2, 0), other(0)),
        lambda: own(2, 1),
        lambda: (own(3, 0), other(1)),
        lambda: own(3, 1),
        lambda: (own(4, 0), other(2)),
        lambda: other(3),
        lambda: other(4),
    )
    before_1 = (
        lambda: other(0),
        lambda: other(1),
        lambda: (own(1, 0), own(1, 1)),
        lambda: (own(2, 0), other(2)),
        lambda: own(2, 1),
        lambda: (own(3, 0), other(3)),
        lambda: own(3, 1),
        lambda: (own(4, 0), other(4)),
    )

    def arrive(k):
        @pl.when(stays)
        def _():
            before_0[k]()

        @pl.when(away)
        def _():
            before_1[k]()

    def attend(t, carry):
        index = jnp.int32(0)
        for k in range(STEPS - 1):
            pl.when(t == k)(functools.partial(arrive, k))
            index = jnp.where(t == k, jnp.where(stays, order_0[k], order_1[k]), index)
        attend_rows(slice(0, T), nall[pl.ds(pl.multiple_of(index * KEYS, KEYS), KEYS)])
        return carry

    def attend_rows(rows, keys):
        s = dot_t(q_v[rows], keys)
        m_old = m_v[rows, 0:1]
        m_new = jnp.maximum(m_old, jnp.max(s, axis=1, keepdims=True))
        p = jnp.exp2(s - m_new)
        alpha = jnp.exp2(m_old - m_new)
        l_new = l_v[rows, 0:1] * alpha + jnp.sum(p, axis=1, keepdims=True)
        l_v[rows] = jnp.broadcast_to(l_new, (l_new.shape[0], 128))
        m_v[rows] = jnp.broadcast_to(m_new, (l_new.shape[0], 128))
        acc_v[rows] = acc_v[rows] * alpha + dot(p.astype(BF), keys)

    lax.fori_loop(0, STEPS - 1, attend, 0)

    frame = col * 2 + h
    home = c * ZS + z

    def a_piece(j, f):
        slot = j // TM
        return pltpu.make_async_remote_copy(
            src_ref=as_t.at[pl.ds(pl.multiple_of(j * PIECE, PIECE), PIECE)],
            dst_ref=tbuf.at[slot, pl.ds(pl.multiple_of(f * PIECE, PIECE), PIECE)],
            send_sem=a_send.at[j], recv_sem=a_recv.at[slot, f],
            device_id=(owner(j), home), device_id_type=MESH,
        )

    def a_local(j):
        slot = j // TM
        return pltpu.make_async_copy(
            as_t.at[pl.ds(pl.multiple_of(j * PIECE, PIECE), PIECE)],
            tbuf.at[slot, pl.ds(pl.multiple_of(frame * PIECE, PIECE), PIECE)],
            a_self.at[slot],
        )

    def is_me(j):
        return jnp.logical_and(stays, owner(j) == tm)

    def a_start(j, carry):
        @pl.when(is_me(j))
        def _():
            a_local(j).start()

        @pl.when(jnp.logical_not(is_me(j)))
        def _():
            a_piece(j, frame).start()

        return carry

    arrive(STEPS - 1)

    for half in range(2):
        part = slice(half * HALF, (half + 1) * HALF)
        attend_rows(part, nall[(STEPS - 1) * KEYS :])
        mixed = (acc_v[part] / l_v[part, 0:1]).astype(BF)
        as_t[part] = (ac_t[part].astype(F32) + dot(mixed, wvo[...])).astype(BF)
        lax.fori_loop(half * (PIECES // 2), (half + 1) * (PIECES // 2), a_start, 0)

    first = lax.rem(13 * tm, TM)
    has_second = first < PIECES - TM

    rows = FRAMES * PIECE
    r_index = lax.broadcasted_iota(jnp.int32, (rows, rows), 0)
    c_index = lax.broadcasted_iota(jnp.int32, (rows, rows), 1)
    allowed = jnp.logical_and((r_index & (PIECE - 1)) == (c_index & (PIECE - 1)), r_index >= c_index)

    def d_piece(slot, j, f):
        return pltpu.make_async_remote_copy(
            src_ref=dbuf.at[slot, pl.ds(pl.multiple_of(f * PIECE, PIECE), PIECE)],
            dst_ref=out.at[pl.ds(pl.multiple_of(j * PIECE, PIECE), PIECE)],
            send_sem=d_send.at[slot, f], recv_sem=d_recv.at[j],
            device_id=(f, sp), device_id_type=MESH,
        )

    def d_local(slot, j):
        return pltpu.make_async_copy(
            dbuf.at[slot, pl.ds(pl.multiple_of(tm * PIECE, PIECE), PIECE)],
            out.at[pl.ds(pl.multiple_of(j * PIECE, PIECE), PIECE)],
            d_self.at[slot],
        )

    def temporal(slot, j):
        def wait_piece(f, carry):
            own = jnp.logical_and(stays, f == frame)

            @pl.when(own)
            def _():
                a_local(j).wait()

            @pl.when(jnp.logical_not(own))
            def _():
                a_piece(slot * TM, f).wait_recv()

            return carry

        lax.fori_loop(0, FRAMES, wait_piece, 0)
        x = tbuf[slot]
        normed = channel_norm(x.astype(F32), gt[...]).astype(BF)
        qv = dot(normed, tw[...]).astype(BF)
        s = jnp.where(allowed, dot_t(qv[:, 0:D], normed), -1e30)
        p = jnp.exp2(s - jnp.max(s, axis=1, keepdims=True))
        total = jnp.sum(p, axis=1, keepdims=True)
        dbuf[slot] = (x.astype(F32) + dot(p.astype(BF), qv[:, D:]) / total).astype(BF)

        def d_start(f, carry):
            @pl.when(f == tm)
            def _():
                d_local(slot, j).start()

            @pl.when(f != tm)
            def _():
                d_piece(slot, j, f).start()

            return carry

        lax.fori_loop(0, FRAMES, d_start, 0)

    temporal(0, first)

    @pl.when(has_second)
    def _():
        temporal(1, TM + first)

    def d_wait(j, carry):
        mine = owner(j) == tm

        @pl.when(mine)
        def _():
            d_local(j // TM, j).wait()

        @pl.when(jnp.logical_not(mine))
        def _():
            d_piece(0, j, tm).wait_recv()

        return carry

    lax.fori_loop(0, PIECES, d_wait, 0)

    def a_sent(j, carry):
        @pl.when(jnp.logical_not(is_me(j)))
        def _():
            a_piece(j, frame).wait_send()

        return carry

    lax.fori_loop(0, PIECES, a_sent, 0)

    def d_sent(f, carry):
        @pl.when(f != tm)
        def _():
            d_piece(0, tm, f).wait_send()

            @pl.when(has_second)
            def _():
                d_piece(1, tm, f).wait_send()

        return carry

    lax.fori_loop(0, FRAMES, d_sent, 0)

    @pl.when(sends_down)
    def _():
        to_down.wait_send()

    @pl.when(sends_up)
    def _():
        to_up.wait_send()

    @pl.when(away)
    def _():
        swap.wait_send()

    for dist in range(ZS // 2 + 1):
        for side in range(2):
            for half in halves(side, dist):
                sib_piece(my_ring, side, dist, half).wait_send()
            for part in parts[side]:
                if travels(side, dist, part):
                    ring_piece(side, dist, part).wait_send()


def local(
    video, gain_conv, conv_weight, gain_space, query_weight, key_weight, value_weight, out_weight,
    gain_time, time_query, time_key, time_value, time_out,
):
    vm = pltpu.VMEM
    dma = pltpu.SemaphoreType.DMA
    decoded = pl.pallas_call(
        kernel,
        out_shape=jax.ShapeDtypeStruct((T, D), BF),
        in_specs=[pl.BlockSpec(memory_space=pl.ANY)] * 13,
        out_specs=pl.BlockSpec(memory_space=pl.ANY),
        scratch_shapes=[
            vm((T, D), BF), vm((2, W, D), BF), vm((1, D), F32), vm((1, D), F32), vm((1, D), F32),
            vm((3, 3 * D, D), BF), *[vm((D, D), BF) for _ in range(9)], vm((D, 2 * D), BF),
            vm((4 * W, 3 * D), BF), vm((T, D), F32), vm((T, D), BF), vm((2 * ZS * T, D), BF),
            vm((T, D), BF), vm((T, 128), F32), vm((T, 128), F32), vm((T, D), F32), vm((T, D), BF),
            vm((2, FRAMES * PIECE, D), BF), vm((2, FRAMES * PIECE, D), BF),
            dma((15,)), dma((2,)), dma((2,)), dma, dma,
            dma((2, 4, 4)), dma((2, 4, 4)), dma((2, 5, 2)), dma((2, 5, 2)),
            dma((PIECES,)), dma((2, FRAMES)), dma((2,)), dma((2, FRAMES)), dma((PIECES,)), dma((2,)),
        ],
        compiler_params=pltpu.CompilerParams(
            collective_id=0, has_side_effects=True, vmem_limit_bytes=56 * 1024 * 1024
        ),
    )(
        video.reshape(T, D), gain_conv.reshape(1, D), conv_weight.reshape(3, 3 * D, D), gain_space.reshape(1, D),
        query_weight, key_weight, value_weight, out_weight, gain_time.reshape(1, D),
        time_query, time_key, time_value, time_out,
    )
    return decoded.reshape(1, 2, W, D)


def solution(mesh):
    return jax.shard_map(
        local,
        mesh=mesh,
        in_specs=(P("tm", "space", None, None),) + (P(),) * 12,
        out_specs=P("tm", "space", None, None),
        check_vma=False,
    )
```

```python
import functools
import math

import jax
import jax.numpy as jnp
from jax import lax
from jax.experimental import pallas as pl
from jax.experimental.pallas import tpu as pltpu
from jax.sharding import PartitionSpec as P

epsilon = 1e-06
MESH = pl.DeviceIdType.MESH
XS, YL, CORES, YH, ZS = 4, 2, 2, 2, 8
TM = XS * YL * CORES
FRAMES = 16
W = 160
D = 512
T = 2 * W
HALF = T // 2
PIECE = 16
PIECES = T // PIECE
SCALE = 1.0 / math.sqrt(D)
LOG2E = math.log2(math.e)
BF = jnp.bfloat16
F32 = jnp.float32

QUARTER = T // 4
KEYS = 2 * T
STEPS = ZS * 2 * T // KEYS


def channel_norm(values, gains):
    average = jnp.mean(values, axis=-1, keepdims=True)
    centered = values - average
    spread = jnp.mean(centered * centered, axis=-1, keepdims=True)
    return centered * lax.rsqrt(spread + epsilon) * gains


def dot(a, b):
    return jnp.dot(a, b, preferred_element_type=F32)


def dot_t(a, b):
    return lax.dot_general(a, b, (((1,), (1,)), ((), ())), preferred_element_type=F32)


def owner(j):
    return lax.rem(5 * j, TM)


def kernel(
    video, gain_conv, conv_w, gain_space, wq, wk, wv, wo, gain_time, tq, tk, tv, to,
    out,
    vid, halo, gc, gs, gt, cw, wq_v, wk_v, wv_v, wo_v, tq_v, tk_v, tv_v, to_v, wvo, tw, tn, tv_n,
    act3, conv_acc, ac_mine, ac_t, n_out, nall, q_v, m_v, l_v, acc_v, as_t, tbuf, dbuf,
    load_sem, halo_send, halo_recv, swap_send, swap_recv,
    ring_send, ring_recv, sib_send, sib_recv,
    a_send, a_recv, a_self, d_send, d_recv, d_self, plane_sem,
):
    tm = lax.axis_index("tm")
    sp = lax.axis_index("space")
    c = lax.rem(tm, 2)
    col = tm // 2
    h = sp // ZS
    z = lax.rem(sp, ZS)
    zp = lax.rem(z + 1, ZS)
    zm = lax.rem(z + ZS - 1, ZS)
    sibling = (col * 2 + 1 - c, sp)
    z_ids = ((tm, h * ZS + zp), (tm, h * ZS + zm))
    stays = c == h
    away = jnp.logical_not(stays)
    work = (col * 2 + h, c * ZS + z)

    loads = []
    for i, (src, dst) in enumerate(
        [
            (video, vid), (gain_conv, gc), (conv_w.at[1], cw.at[1]), (conv_w.at[0], cw.at[0]),
            (conv_w.at[2], cw.at[2]), (gain_space, gs), (wq, wq_v), (wk, wk_v), (wv, wv_v), (wo, wo_v),
            (gain_time, gt), (tq, tq_v), (tk, tk_v), (tv, tv_v), (to, to_v),
        ]
    ):
        loads.append(pltpu.make_async_copy(src, dst, load_sem.at[i]))
    for load in loads[:6]:
        load.start()

    barrier = pltpu.get_barrier_semaphore()

    def greet(i, carry):
        other_c, other_h = lax.rem(i, 2), i // 2

        @pl.when(jnp.logical_or(other_c != c, other_h != h))
        def _():
            other = (col * 2 + other_c, other_h * ZS + z)
            pl.semaphore_signal(barrier, inc=1, device_id=other, device_id_type=MESH)

        for other_z in (zp, zm):
            other = (col * 2 + other_c, other_h * ZS + other_z)
            pl.semaphore_signal(barrier, inc=1, device_id=other, device_id_type=MESH)
        return carry

    lax.fori_loop(0, CORES * YH, greet, 0)
    flips = [(tm + 2 * bit - 4 * bit * lax.rem(col // bit, 2), sp) for bit in (1, 2, 4)]
    for flip in flips:
        pl.semaphore_signal(barrier, inc=1, device_id=flip, device_id_type=MESH)
    pl.semaphore_wait(barrier, 3 * CORES * YH - 1 + len(flips))

    def hear(k):
        if k:
            pl.semaphore_wait(plane_sem.at[k - 1], 1)
        if k < len(flips):
            pl.semaphore_signal(plane_sem.at[k], inc=1, device_id=flips[k], device_id_type=MESH)

    hear(0)

    has_up = sp > 0
    has_down = sp < YH * ZS - 1
    to_down = pltpu.make_async_remote_copy(
        src_ref=video.at[pl.ds(W, W)], dst_ref=halo.at[0], send_sem=halo_send.at[0], recv_sem=halo_recv.at[0],
        device_id=(tm, jnp.minimum(sp + 1, YH * ZS - 1)), device_id_type=MESH,
    )
    to_up = pltpu.make_async_remote_copy(
        src_ref=video.at[pl.ds(0, W)], dst_ref=halo.at[1], send_sem=halo_send.at[1], recv_sem=halo_recv.at[1],
        device_id=(tm, jnp.maximum(sp - 1, 0)), device_id_type=MESH,
    )

    @pl.when(has_down)
    def _():
        to_down.start()

    @pl.when(has_up)
    def _():
        to_up.start()

    for load in loads[6:]:
        load.start()
    loads[0].wait()
    loads[1].wait()
    col_index = lax.broadcasted_iota(jnp.int32, (W, D), 0)

    def activate(row, raw):
        u = channel_norm(raw.astype(F32), gc[...])
        u = (u / (1.0 + jnp.exp(-u))).astype(BF).astype(F32)
        left = jnp.where(col_index == 0, 0.0, pltpu.roll(u, 1, 0))
        right = jnp.where(col_index == W - 1, 0.0, pltpu.roll(u, W - 1, 0))
        act3[pl.ds(row * W, W), 0:D] = left.astype(BF)
        act3[pl.ds(row * W, W), D : 2 * D] = u.astype(BF)
        act3[pl.ds(row * W, W), 2 * D : 3 * D] = right.astype(BF)

    activate(1, vid[0:W])
    activate(2, vid[W:T])
    loads[2].wait()
    conv_acc[...] = vid[...].astype(F32) + dot(act3[W : 3 * W], cw[1])
    loads[3].wait()
    conv_acc[W:T] += dot(act3[W : 2 * W], cw[0])
    loads[4].wait()
    conv_acc[0:W] += dot(act3[2 * W : 3 * W], cw[2])

    my_ring = jnp.where(stays, 0, 1)

    def place_of(ring, side, dist):
        if dist == 0:
            return ring * T
        if dist == ZS // 2:
            return (4 * dist - 2 + ring) * T
        return (4 * dist - 2 + 2 * ring + side) * T

    def rows_of(ring, side, dist, start, size):
        return nall.at[pl.ds(pl.multiple_of(place_of(ring, side, dist) + start, PIECE), size)]

    def ring_piece(side, dist, part):
        return pltpu.make_async_remote_copy(
            src_ref=rows_of(my_ring, side, dist, part * QUARTER, QUARTER),
            dst_ref=rows_of(my_ring, side, dist + 1, part * QUARTER, QUARTER),
            send_sem=ring_send.at[side, dist, part], recv_sem=ring_recv.at[side, dist, part],
            device_id=z_ids[side], device_id_type=MESH,
        )

    def swap_piece(part):
        return pltpu.make_async_remote_copy(
            src_ref=n_out.at[pl.ds(part * QUARTER, QUARTER)], dst_ref=rows_of(1, 0, 0, part * QUARTER, QUARTER),
            send_sem=swap_send.at[part], recv_sem=swap_recv.at[part], device_id=work, device_id_type=MESH,
        )

    swap_conv = pltpu.make_async_remote_copy(
        src_ref=ac_mine, dst_ref=ac_t, send_sem=swap_send.at[4], recv_sem=swap_recv.at[4],
        device_id=work, device_id_type=MESH,
    )

    def sib_piece(ring, side, dist, half):
        ref = rows_of(ring, side, dist, half * HALF, HALF)
        return pltpu.make_async_remote_copy(
            src_ref=ref, dst_ref=ref, send_sem=sib_send.at[side, dist, half], recv_sem=sib_recv.at[side, dist, half],
            device_id=sibling, device_id_type=MESH,
        )

    parts = ((0, 1, 2, 3), (2, 3, 0, 1))

    def travels(side, dist, part):
        return dist < ZS // 2 - 1 or (dist == ZS // 2 - 1 and part // 2 == side)

    def halves(side, dist):
        if dist == 0:
            return (0, 1) if side == 0 else ()
        return (side, 1 - side) if dist < ZS // 2 else (side,)

    def finish_row(row, arrives, copy, tap):
        part = slice(row * W, (row + 1) * W)

        @pl.when(arrives)
        def _():
            copy.wait_recv()
            activate(3 * row, halo[row])
            conv_acc[part] += dot(act3[3 * row * W : (3 * row + 1) * W], cw[tap])

        after_conv = conv_acc[part].astype(BF)
        normed = channel_norm(after_conv.astype(F32), gs[...]).astype(BF)

        @pl.when(stays)
        def _():
            ac_t[part] = after_conv
            nall[part] = normed
            for quarter in (2 * row, 2 * row + 1):
                for side in range(2):
                    ring_piece(side, 0, quarter).start()
            sib_piece(0, 0, 0, row).start()

        @pl.when(away)
        def _():
            ac_mine[part] = after_conv
            n_out[part] = normed
            for quarter in (2 * row, 2 * row + 1):
                swap_piece(quarter).start()

    loads[5].wait()
    finish_row(0, has_up, to_down, 0)
    finish_row(1, has_down, to_up, 2)

    hear(1)

    for i in range(6, 15):
        loads[i].wait()
    wvo[...] = dot(wv_v[...], wo_v[...]).astype(BF)
    tw[:, 0:D] = (dot_t(tq_v[...], tk_v[...]) * (SCALE * LOG2E)).astype(BF)
    tw[:, D : 2 * D] = dot(tv_v[...], to_v[...]).astype(BF)

    @pl.when(away)
    def _():
        for part in range(4):
            swap_piece(part).wait_recv()
            for side in range(2):
                ring_piece(side, 0, part).start()
            if part % 2 == 1:
                sib_piece(1, 0, 0, part // 2).start()

    query = dot(nall[pl.ds(pl.multiple_of(my_ring * T, T), T)], wq_v[...]).astype(BF)
    q_v[...] = (dot_t(query, wk_v[...]) * (SCALE * LOG2E)).astype(BF)
    m_v[...] = jnp.full(m_v.shape, -1e30, F32)
    l_v[...] = jnp.zeros(l_v.shape, F32)
    acc_v[...] = jnp.zeros(acc_v.shape, F32)

    def own(dist, half):
        if dist == ZS // 2 and half == 1:
            return
        for i in (2 * half, 2 * half + 1):
            for side in range(2):
                part = parts[side][i]
                ring_piece(side, dist - 1, part).wait_recv()
                if travels(side, dist, part):
                    ring_piece(side, dist, part).start()
        for side in range(2):
            sib_piece(my_ring, side, dist, halves(side, dist)[half]).start()

    def other(dist):
        for side in range(2):
            for half in halves(side, dist):
                sib_piece(1 - my_ring, side, dist, half).wait_recv()

    order_0 = (1, 0, 3, 2, 5, 4, 6, 7)
    order_1 = (0, 1, 2, 3, 4, 5, 6, 7)
    before_0 = (
        lambda: (own(1, 0), own(1, 1)),
        lambda: (own(2, 0), other(0)),
        lambda: own(2, 1),
        lambda: (own(3, 0), other(1)),
        lambda: own(3, 1),
        lambda: (own(4, 0), other(2)),
        lambda: other(3),
        lambda: other(4),
    )
    before_1 = (
        lambda: other(0),
        lambda: other(1),
        lambda: (own(1, 0), own(1, 1), swap_conv.start()),
        lambda: (own(2, 0), other(2)),
        lambda: own(2, 1),
        lambda: (own(3, 0), other(3)),
        lambda: own(3, 1),
        lambda: (own(4, 0), other(4)),
    )

    def arrive(k):
        @pl.when(stays)
        def _():
            before_0[k]()

        @pl.when(away)
        def _():
            before_1[k]()

    def attend(t, carry):
        index = jnp.int32(0)
        for k in range(STEPS - 1):
            pl.when(t == k)(functools.partial(arrive, k))
            index = jnp.where(t == k, jnp.where(stays, order_0[k], order_1[k]), index)
        attend_rows(slice(0, T), nall[pl.ds(pl.multiple_of(index * KEYS, KEYS), KEYS)])
        return carry

    def attend_rows(rows, keys):
        s = dot_t(q_v[rows], keys)
        m_old = m_v[rows, 0:1]
        m_new = jnp.maximum(m_old, jnp.max(s, axis=1, keepdims=True))
        p = jnp.exp2(s - m_new)
        alpha = jnp.exp2(m_old - m_new)
        l_new = l_v[rows, 0:1] * alpha + jnp.sum(p, axis=1, keepdims=True)
        l_v[rows] = jnp.broadcast_to(l_new, (l_new.shape[0], 128))
        m_v[rows] = jnp.broadcast_to(m_new, (l_new.shape[0], 128))
        acc_v[rows] = acc_v[rows] * alpha + dot(p.astype(BF), keys)

    hear(2)
    lax.fori_loop(0, STEPS - 1, attend, 0)
    hear(3)

    frame = col * 2 + h
    home = c * ZS + z

    def a_piece(j, f):
        slot = j // TM
        return pltpu.make_async_remote_copy(
            src_ref=as_t.at[pl.ds(pl.multiple_of(j * PIECE, PIECE), PIECE)],
            dst_ref=tbuf.at[slot, pl.ds(pl.multiple_of(f * PIECE, PIECE), PIECE)],
            send_sem=a_send.at[j], recv_sem=a_recv.at[slot, f],
            device_id=(owner(j), home), device_id_type=MESH,
        )

    def a_local(j):
        slot = j // TM
        return pltpu.make_async_copy(
            as_t.at[pl.ds(pl.multiple_of(j * PIECE, PIECE), PIECE)],
            tbuf.at[slot, pl.ds(pl.multiple_of(frame * PIECE, PIECE), PIECE)],
            a_self.at[slot],
        )

    def is_me(j):
        return jnp.logical_and(stays, owner(j) == tm)

    def a_start(j, carry):
        @pl.when(is_me(j))
        def _():
            a_local(j).start()

        @pl.when(jnp.logical_not(is_me(j)))
        def _():
            a_piece(j, frame).start()

        return carry

    arrive(STEPS - 1)

    @pl.when(away)
    def _():
        swap_conv.wait_recv()

    for start, stop in ((0, 6), (6, PIECES)):
        part = slice(start * PIECE, stop * PIECE)
        attend_rows(part, nall[(STEPS - 1) * KEYS :])
        mixed = (acc_v[part] / l_v[part, 0:1]).astype(BF)
        as_t[part] = (ac_t[part].astype(F32) + dot(mixed, wvo[...])).astype(BF)
        lax.fori_loop(start, stop, a_start, 0)

    first = lax.rem(13 * tm, TM)
    has_second = first < PIECES - TM

    rows = FRAMES * PIECE
    r_index = lax.broadcasted_iota(jnp.int32, (rows, rows), 0)
    c_index = lax.broadcasted_iota(jnp.int32, (rows, rows), 1)
    allowed = jnp.logical_and((r_index & (PIECE - 1)) == (c_index & (PIECE - 1)), r_index >= c_index)

    def d_piece(slot, j, f):
        return pltpu.make_async_remote_copy(
            src_ref=dbuf.at[slot, pl.ds(pl.multiple_of(f * PIECE, PIECE), PIECE)],
            dst_ref=out.at[pl.ds(pl.multiple_of(j * PIECE, PIECE), PIECE)],
            send_sem=d_send.at[slot, f], recv_sem=d_recv.at[j],
            device_id=(f, sp), device_id_type=MESH,
        )

    def d_local(slot, j):
        return pltpu.make_async_copy(
            dbuf.at[slot, pl.ds(pl.multiple_of(tm * PIECE, PIECE), PIECE)],
            out.at[pl.ds(pl.multiple_of(j * PIECE, PIECE), PIECE)],
            d_self.at[slot],
        )

    def temporal(slot, j):
        def wait_piece(f, carry):
            own = jnp.logical_and(stays, f == frame)

            @pl.when(own)
            def _():
                a_local(j).wait()

            @pl.when(jnp.logical_not(own))
            def _():
                a_piece(slot * TM, f).wait_recv()

            return carry

        def d_start(f, carry):
            @pl.when(f == tm)
            def _():
                d_local(slot, j).start()

            @pl.when(f != tm)
            def _():
                d_piece(slot, j, f).start()

            return carry

        middle = rows // 2
        for begin, end in ((0, middle), (middle, rows)):
            lax.fori_loop(begin // PIECE, end // PIECE, wait_piece, 0)
            x = tbuf[slot, begin:end]
            normed = channel_norm(x.astype(F32), gt[...]).astype(BF)
            qv = dot(normed, tw[...]).astype(BF)
            tn[begin:end] = normed
            tv_n[begin:end] = qv[:, D:]
            s = jnp.where(allowed[begin:end, 0:end], dot_t(qv[:, 0:D], tn[0:end]), -1e30)
            p = jnp.exp2(s - jnp.max(s, axis=1, keepdims=True))
            total = jnp.sum(p, axis=1, keepdims=True)
            dbuf[slot, begin:end] = (x.astype(F32) + dot(p.astype(BF), tv_n[0:end]) / total).astype(BF)
            lax.fori_loop(begin // PIECE, end // PIECE, d_start, 0)

    temporal(0, first)

    @pl.when(has_second)
    def _():
        temporal(1, TM + first)

    def d_wait(j, carry):
        mine = owner(j) == tm

        @pl.when(mine)
        def _():
            d_local(j // TM, j).wait()

        @pl.when(jnp.logical_not(mine))
        def _():
            d_piece(0, j, tm).wait_recv()

        return carry

    lax.fori_loop(0, PIECES, d_wait, 0)

    def a_sent(j, carry):
        @pl.when(jnp.logical_not(is_me(j)))
        def _():
            a_piece(j, frame).wait_send()

        return carry

    lax.fori_loop(0, PIECES, a_sent, 0)

    def d_sent(f, carry):
        @pl.when(f != tm)
        def _():
            d_piece(0, tm, f).wait_send()

            @pl.when(has_second)
            def _():
                d_piece(1, tm, f).wait_send()

        return carry

    lax.fori_loop(0, FRAMES, d_sent, 0)

    @pl.when(has_down)
    def _():
        to_down.wait_send()

    @pl.when(has_up)
    def _():
        to_up.wait_send()

    @pl.when(away)
    def _():
        swap_conv.wait_send()
        for part in range(4):
            swap_piece(part).wait_send()

    for dist in range(ZS // 2 + 1):
        for side in range(2):
            for half in halves(side, dist):
                sib_piece(my_ring, side, dist, half).wait_send()
            for part in parts[side]:
                if travels(side, dist, part):
                    ring_piece(side, dist, part).wait_send()


def local(
    video, gain_conv, conv_weight, gain_space, query_weight, key_weight, value_weight, out_weight,
    gain_time, time_query, time_key, time_value, time_out,
):
    vm = pltpu.VMEM
    dma = pltpu.SemaphoreType.DMA
    decoded = pl.pallas_call(
        kernel,
        out_shape=jax.ShapeDtypeStruct((T, D), BF),
        in_specs=[pl.BlockSpec(memory_space=pl.ANY)] * 13,
        out_specs=pl.BlockSpec(memory_space=pl.ANY),
        scratch_shapes=[
            vm((T, D), BF), vm((2, W, D), BF), vm((1, D), F32), vm((1, D), F32), vm((1, D), F32),
            vm((3, 3 * D, D), BF), *[vm((D, D), BF) for _ in range(9)], vm((D, 2 * D), BF), vm((FRAMES * PIECE, D), BF), vm((FRAMES * PIECE, D), BF),
            vm((4 * W, 3 * D), BF), vm((T, D), F32), vm((T, D), BF), vm((T, D), BF), vm((T, D), BF), vm((2 * ZS * T, D), BF),
            vm((T, D), BF), vm((T, 128), F32), vm((T, 128), F32), vm((T, D), F32), vm((T, D), BF),
            vm((2, FRAMES * PIECE, D), BF), vm((2, FRAMES * PIECE, D), BF),
            dma((15,)), dma((2,)), dma((2,)), dma((5,)), dma((5,)),
            dma((2, 4, 4)), dma((2, 4, 4)), dma((2, 5, 2)), dma((2, 5, 2)),
            dma((PIECES,)), dma((2, FRAMES)), dma((2,)), dma((2, FRAMES)), dma((PIECES,)), dma((2,)), pltpu.SemaphoreType.REGULAR((3,)),
        ],
        compiler_params=pltpu.CompilerParams(
            collective_id=0, has_side_effects=True, vmem_limit_bytes=56 * 1024 * 1024
        ),
    )(
        video.reshape(T, D), gain_conv.reshape(1, D), conv_weight.reshape(3, 3 * D, D), gain_space.reshape(1, D),
        query_weight, key_weight, value_weight, out_weight, gain_time.reshape(1, D),
        time_query, time_key, time_value, time_out,
    )
    return decoded.reshape(1, 2, W, D)


def solution(mesh):
    return jax.shard_map(
        local,
        mesh=mesh,
        in_specs=(P("tm", "space", None, None),) + (P(),) * 12,
        out_specs=P("tm", "space", None, None),
        check_vma=False,
    )
```

```python
import functools
import math

import jax
import jax.numpy as jnp
from jax import lax
from jax.experimental import pallas as pl
from jax.experimental.pallas import tpu as pltpu
from jax.sharding import PartitionSpec as P

epsilon = 1e-06
MESH = pl.DeviceIdType.MESH
XS, YL, CORES, YH, ZS = 4, 2, 2, 2, 8
TM = XS * YL * CORES
FRAMES = 16
W = 160
D = 512
T = 2 * W
HALF = T // 2
PIECE = 16
PIECES = T // PIECE
SCALE = 1.0 / math.sqrt(D)
LOG2E = math.log2(math.e)
BF = jnp.bfloat16
F32 = jnp.float32

QUARTER = T // 4
KEYS = 2 * T
STEPS = ZS * 2 * T // KEYS


def channel_norm(values, gains):
    average = jnp.mean(values, axis=-1, keepdims=True)
    centered = values - average
    spread = jnp.mean(centered * centered, axis=-1, keepdims=True)
    return centered * lax.rsqrt(spread + epsilon) * gains


def dot(a, b):
    return jnp.dot(a, b, preferred_element_type=F32)


def dot_t(a, b):
    return lax.dot_general(a, b, (((1,), (1,)), ((), ())), preferred_element_type=F32)


def owner(j):
    return lax.rem(5 * j, TM)


def kernel(
    video, gain_conv, conv_w, gain_space, wq, wk, wv, wo, gain_time, tq, tk, tv, to,
    out,
    vid, halo, gc, gs, gt, cw, wq_v, wk_v, wv_v, wo_v, tq_v, tk_v, tv_v, to_v, wvo, tw, tn, tv_n,
    act3, conv_acc, ac_mine, ac_t, n_out, nall, q_v, m_v, l_v, acc_v, as_t, tbuf, dbuf,
    load_sem, halo_send, halo_recv, swap_send, swap_recv,
    ring_send, ring_recv, sib_send, sib_recv,
    a_send, a_recv, a_self, d_send, d_recv, d_self, plane_sem,
):
    tm = lax.axis_index("tm")
    sp = lax.axis_index("space")
    c = lax.rem(tm, 2)
    col = tm // 2
    h = sp // ZS
    z = lax.rem(sp, ZS)
    zp = lax.rem(z + 1, ZS)
    zm = lax.rem(z + ZS - 1, ZS)
    sibling = (col * 2 + 1 - c, sp)
    z_ids = ((tm, h * ZS + zp), (tm, h * ZS + zm))
    stays = c == h
    away = jnp.logical_not(stays)
    work = (col * 2 + h, c * ZS + z)

    barrier = pltpu.get_barrier_semaphore()
    flips = [(tm + 2 * bit - 4 * bit * lax.rem(col // bit, 2), sp) for bit in (1, 2, 4)]
    across = (tm, (1 - h) * ZS + z)
    near = [*z_ids, sibling, across, (sibling[0], across[1]), *flips]
    for other in near:
        pl.semaphore_signal(barrier, inc=1, device_id=other, device_id_type=MESH)
    crosses = jnp.logical_or(sp == ZS - 1, sp == ZS)

    @pl.when(crosses)
    def _():
        other = (tm, 2 * ZS - 1 - sp)
        pl.semaphore_signal(barrier, inc=1, device_id=other, device_id_type=MESH)

    loads = []
    for i, (src, dst) in enumerate(
        [
            (video, vid), (gain_conv, gc), (conv_w.at[1], cw.at[1]), (conv_w.at[0], cw.at[0]),
            (conv_w.at[2], cw.at[2]), (gain_space, gs), (wq, wq_v), (wk, wk_v), (wv, wv_v), (wo, wo_v),
            (gain_time, gt), (tq, tq_v), (tk, tk_v), (tv, tv_v), (to, to_v),
        ]
    ):
        loads.append(pltpu.make_async_copy(src, dst, load_sem.at[i]))
    for load in loads[:6]:
        load.start()

    pl.semaphore_wait(barrier, len(near) + jnp.where(crosses, 1, 0))

    def hear(k):
        if k:
            pl.semaphore_wait(plane_sem.at[k - 1], 1)
        if k < len(flips):
            pl.semaphore_signal(plane_sem.at[k], inc=1, device_id=flips[k], device_id_type=MESH)

    hear(0)

    has_up = sp > 0
    has_down = sp < YH * ZS - 1
    to_down = pltpu.make_async_remote_copy(
        src_ref=video.at[pl.ds(W, W)], dst_ref=halo.at[0], send_sem=halo_send.at[0], recv_sem=halo_recv.at[0],
        device_id=(tm, jnp.minimum(sp + 1, YH * ZS - 1)), device_id_type=MESH,
    )
    to_up = pltpu.make_async_remote_copy(
        src_ref=video.at[pl.ds(0, W)], dst_ref=halo.at[1], send_sem=halo_send.at[1], recv_sem=halo_recv.at[1],
        device_id=(tm, jnp.maximum(sp - 1, 0)), device_id_type=MESH,
    )

    @pl.when(has_down)
    def _():
        to_down.start()

    @pl.when(has_up)
    def _():
        to_up.start()

    for load in loads[6:]:
        load.start()
    loads[0].wait()
    loads[1].wait()
    col_index = lax.broadcasted_iota(jnp.int32, (W, D), 0)

    def activate(row, raw):
        u = channel_norm(raw.astype(F32), gc[...])
        u = (u / (1.0 + jnp.exp(-u))).astype(BF).astype(F32)
        left = jnp.where(col_index == 0, 0.0, pltpu.roll(u, 1, 0))
        right = jnp.where(col_index == W - 1, 0.0, pltpu.roll(u, W - 1, 0))
        act3[pl.ds(row * W, W), 0:D] = left.astype(BF)
        act3[pl.ds(row * W, W), D : 2 * D] = u.astype(BF)
        act3[pl.ds(row * W, W), 2 * D : 3 * D] = right.astype(BF)

    activate(1, vid[0:W])
    activate(2, vid[W:T])
    loads[2].wait()
    conv_acc[...] = vid[...].astype(F32) + dot(act3[W : 3 * W], cw[1])
    loads[3].wait()
    conv_acc[W:T] += dot(act3[W : 2 * W], cw[0])
    loads[4].wait()
    conv_acc[0:W] += dot(act3[2 * W : 3 * W], cw[2])

    my_ring = jnp.where(stays, 0, 1)

    def place_of(ring, side, dist):
        if dist == 0:
            return ring * T
        if dist == ZS // 2:
            return (4 * dist - 2 + ring) * T
        return (4 * dist - 2 + 2 * ring + side) * T

    def rows_of(ring, side, dist, start, size):
        return nall.at[pl.ds(pl.multiple_of(place_of(ring, side, dist) + start, PIECE), size)]

    def ring_piece(side, dist, part):
        return pltpu.make_async_remote_copy(
            src_ref=rows_of(my_ring, side, dist, part * QUARTER, QUARTER),
            dst_ref=rows_of(my_ring, side, dist + 1, part * QUARTER, QUARTER),
            send_sem=ring_send.at[side, dist, part], recv_sem=ring_recv.at[side, dist, part],
            device_id=z_ids[side], device_id_type=MESH,
        )

    def swap_piece(part):
        return pltpu.make_async_remote_copy(
            src_ref=n_out.at[pl.ds(part * QUARTER, QUARTER)], dst_ref=rows_of(1, 0, 0, part * QUARTER, QUARTER),
            send_sem=swap_send.at[part], recv_sem=swap_recv.at[part], device_id=work, device_id_type=MESH,
        )

    swap_conv = pltpu.make_async_remote_copy(
        src_ref=ac_mine, dst_ref=ac_t, send_sem=swap_send.at[4], recv_sem=swap_recv.at[4],
        device_id=work, device_id_type=MESH,
    )

    def sib_piece(ring, side, dist, half):
        ref = rows_of(ring, side, dist, half * HALF, HALF)
        return pltpu.make_async_remote_copy(
            src_ref=ref, dst_ref=ref, send_sem=sib_send.at[side, dist, half], recv_sem=sib_recv.at[side, dist, half],
            device_id=sibling, device_id_type=MESH,
        )

    parts = ((0, 1, 2, 3), (2, 3, 0, 1))

    def travels(side, dist, part):
        return dist < ZS // 2 - 1 or (dist == ZS // 2 - 1 and part // 2 == side)

    def halves(side, dist):
        if dist == 0:
            return (0, 1) if side == 0 else ()
        return (side, 1 - side) if dist < ZS // 2 else (side,)

    def finish_row(row, arrives, copy, tap):
        part = slice(row * W, (row + 1) * W)

        @pl.when(arrives)
        def _():
            copy.wait_recv()
            activate(3 * row, halo[row])
            conv_acc[part] += dot(act3[3 * row * W : (3 * row + 1) * W], cw[tap])

        after_conv = conv_acc[part].astype(BF)
        normed = channel_norm(after_conv.astype(F32), gs[...]).astype(BF)

        @pl.when(stays)
        def _():
            ac_t[part] = after_conv
            nall[part] = normed
            for quarter in (2 * row, 2 * row + 1):
                for side in range(2):
                    ring_piece(side, 0, quarter).start()
            sib_piece(0, 0, 0, row).start()

        @pl.when(away)
        def _():
            ac_mine[part] = after_conv
            n_out[part] = normed
            for quarter in (2 * row, 2 * row + 1):
                swap_piece(quarter).start()

    loads[5].wait()
    finish_row(0, has_up, to_down, 0)
    finish_row(1, has_down, to_up, 2)

    hear(1)

    for i in range(6, 15):
        loads[i].wait()
    wvo[...] = dot(wv_v[...], wo_v[...]).astype(BF)
    tw[:, 0:D] = (dot_t(tq_v[...], tk_v[...]) * (SCALE * LOG2E)).astype(BF)
    tw[:, D : 2 * D] = dot(tv_v[...], to_v[...]).astype(BF)

    @pl.when(away)
    def _():
        for part in range(4):
            swap_piece(part).wait_recv()
            for side in range(2):
                ring_piece(side, 0, part).start()
            if part % 2 == 1:
                sib_piece(1, 0, 0, part // 2).start()

    query = dot(nall[pl.ds(pl.multiple_of(my_ring * T, T), T)], wq_v[...]).astype(BF)
    q_v[...] = (dot_t(query, wk_v[...]) * (SCALE * LOG2E)).astype(BF)
    m_v[...] = jnp.full(m_v.shape, -1e30, F32)
    l_v[...] = jnp.zeros(l_v.shape, F32)
    acc_v[...] = jnp.zeros(acc_v.shape, F32)

    def own(dist, half):
        if dist == ZS // 2 and half == 1:
            return
        for i in (2 * half, 2 * half + 1):
            for side in range(2):
                part = parts[side][i]
                ring_piece(side, dist - 1, part).wait_recv()
                if travels(side, dist, part):
                    ring_piece(side, dist, part).start()
        for side in range(2):
            sib_piece(my_ring, side, dist, halves(side, dist)[half]).start()

    def other(dist):
        for side in range(2):
            for half in halves(side, dist):
                sib_piece(1 - my_ring, side, dist, half).wait_recv()

    order_0 = (1, 0, 3, 2, 5, 4, 6, 7)
    order_1 = (0, 1, 2, 3, 4, 5, 6, 7)
    before_0 = (
        lambda: (own(1, 0), own(1, 1)),
        lambda: (own(2, 0), other(0)),
        lambda: own(2, 1),
        lambda: (own(3, 0), other(1)),
        lambda: own(3, 1),
        lambda: (own(4, 0), other(2)),
        lambda: other(3),
        lambda: other(4),
    )
    before_1 = (
        lambda: other(0),
        lambda: other(1),
        lambda: (own(1, 0), own(1, 1), swap_conv.start()),
        lambda: (own(2, 0), other(2)),
        lambda: own(2, 1),
        lambda: (own(3, 0), other(3)),
        lambda: own(3, 1),
        lambda: (own(4, 0), other(4)),
    )

    def arrive(k):
        @pl.when(stays)
        def _():
            before_0[k]()

        @pl.when(away)
        def _():
            before_1[k]()

    def attend(t, carry):
        index = jnp.int32(0)
        for k in range(STEPS - 1):
            pl.when(t == k)(functools.partial(arrive, k))
            index = jnp.where(t == k, jnp.where(stays, order_0[k], order_1[k]), index)
        attend_rows(slice(0, T), nall[pl.ds(pl.multiple_of(index * KEYS, KEYS), KEYS)])
        return carry

    def attend_rows(rows, keys):
        s = dot_t(q_v[rows], keys)
        m_old = m_v[rows, 0:1]
        m_new = jnp.maximum(m_old, jnp.max(s, axis=1, keepdims=True))
        p = jnp.exp2(s - m_new)
        alpha = jnp.exp2(m_old - m_new)
        l_new = l_v[rows, 0:1] * alpha + jnp.sum(p, axis=1, keepdims=True)
        l_v[rows] = jnp.broadcast_to(l_new, (l_new.shape[0], 128))
        m_v[rows] = jnp.broadcast_to(m_new, (l_new.shape[0], 128))
        acc_v[rows] = acc_v[rows] * alpha + dot(p.astype(BF), keys)

    hear(2)
    lax.fori_loop(0, STEPS - 1, attend, 0)
    hear(3)

    frame = col * 2 + h
    home = c * ZS + z

    def a_piece(j, f):
        slot = j // TM
        return pltpu.make_async_remote_copy(
            src_ref=as_t.at[pl.ds(pl.multiple_of(j * PIECE, PIECE), PIECE)],
            dst_ref=tbuf.at[slot, pl.ds(pl.multiple_of(f * PIECE, PIECE), PIECE)],
            send_sem=a_send.at[j], recv_sem=a_recv.at[slot, f],
            device_id=(owner(j), home), device_id_type=MESH,
        )

    def a_local(j):
        slot = j // TM
        return pltpu.make_async_copy(
            as_t.at[pl.ds(pl.multiple_of(j * PIECE, PIECE), PIECE)],
            tbuf.at[slot, pl.ds(pl.multiple_of(frame * PIECE, PIECE), PIECE)],
            a_self.at[slot],
        )

    def is_me(j):
        return jnp.logical_and(stays, owner(j) == tm)

    def a_start(j, carry):
        @pl.when(is_me(j))
        def _():
            a_local(j).start()

        @pl.when(jnp.logical_not(is_me(j)))
        def _():
            a_piece(j, frame).start()

        return carry

    arrive(STEPS - 1)

    @pl.when(away)
    def _():
        swap_conv.wait_recv()

    for start, stop in ((0, 6), (6, PIECES)):
        part = slice(start * PIECE, stop * PIECE)
        attend_rows(part, nall[(STEPS - 1) * KEYS :])
        mixed = (acc_v[part] / l_v[part, 0:1]).astype(BF)
        as_t[part] = (ac_t[part].astype(F32) + dot(mixed, wvo[...])).astype(BF)
        lax.fori_loop(start, stop, a_start, 0)

    first = lax.rem(13 * tm, TM)
    has_second = first < PIECES - TM

    rows = FRAMES * PIECE
    r_index = lax.broadcasted_iota(jnp.int32, (rows, rows), 0)
    c_index = lax.broadcasted_iota(jnp.int32, (rows, rows), 1)
    allowed = jnp.logical_and((r_index & (PIECE - 1)) == (c_index & (PIECE - 1)), r_index >= c_index)

    def d_piece(slot, j, f):
        return pltpu.make_async_remote_copy(
            src_ref=dbuf.at[slot, pl.ds(pl.multiple_of(f * PIECE, PIECE), PIECE)],
            dst_ref=out.at[pl.ds(pl.multiple_of(j * PIECE, PIECE), PIECE)],
            send_sem=d_send.at[slot, f], recv_sem=d_recv.at[j],
            device_id=(f, sp), device_id_type=MESH,
        )

    def d_local(slot, j):
        return pltpu.make_async_copy(
            dbuf.at[slot, pl.ds(pl.multiple_of(tm * PIECE, PIECE), PIECE)],
            out.at[pl.ds(pl.multiple_of(j * PIECE, PIECE), PIECE)],
            d_self.at[slot],
        )

    def temporal(slot, j):
        def wait_piece(f, carry):
            own = jnp.logical_and(stays, f == frame)

            @pl.when(own)
            def _():
                a_local(j).wait()

            @pl.when(jnp.logical_not(own))
            def _():
                a_piece(slot * TM, f).wait_recv()

            return carry

        def d_start(f, carry):
            @pl.when(f == tm)
            def _():
                d_local(slot, j).start()

            @pl.when(f != tm)
            def _():
                d_piece(slot, j, f).start()

            return carry

        middle = rows // 2
        for begin, end in ((0, middle), (middle, rows)):
            lax.fori_loop(begin // PIECE, end // PIECE, wait_piece, 0)
            x = tbuf[slot, begin:end]
            normed = channel_norm(x.astype(F32), gt[...]).astype(BF)
            qv = dot(normed, tw[...]).astype(BF)
            tn[begin:end] = normed
            tv_n[begin:end] = qv[:, D:]
            s = jnp.where(allowed[begin:end, 0:end], dot_t(qv[:, 0:D], tn[0:end]), -1e30)
            p = jnp.exp2(s - jnp.max(s, axis=1, keepdims=True))
            total = jnp.sum(p, axis=1, keepdims=True)
            dbuf[slot, begin:end] = (x.astype(F32) + dot(p.astype(BF), tv_n[0:end]) / total).astype(BF)
            lax.fori_loop(begin // PIECE, end // PIECE, d_start, 0)

    temporal(0, first)

    @pl.when(has_second)
    def _():
        temporal(1, TM + first)

    def d_wait(j, carry):
        mine = owner(j) == tm

        @pl.when(mine)
        def _():
            d_local(j // TM, j).wait()

        @pl.when(jnp.logical_not(mine))
        def _():
            d_piece(0, j, tm).wait_recv()

        return carry

    lax.fori_loop(0, PIECES, d_wait, 0)

    def a_sent(j, carry):
        @pl.when(jnp.logical_not(is_me(j)))
        def _():
            a_piece(j, frame).wait_send()

        return carry

    lax.fori_loop(0, PIECES, a_sent, 0)

    def d_sent(f, carry):
        @pl.when(f != tm)
        def _():
            d_piece(0, tm, f).wait_send()

            @pl.when(has_second)
            def _():
                d_piece(1, tm, f).wait_send()

        return carry

    lax.fori_loop(0, FRAMES, d_sent, 0)

    @pl.when(has_down)
    def _():
        to_down.wait_send()

    @pl.when(has_up)
    def _():
        to_up.wait_send()

    @pl.when(away)
    def _():
        swap_conv.wait_send()
        for part in range(4):
            swap_piece(part).wait_send()

    for dist in range(ZS // 2 + 1):
        for side in range(2):
            for half in halves(side, dist):
                sib_piece(my_ring, side, dist, half).wait_send()
            for part in parts[side]:
                if travels(side, dist, part):
                    ring_piece(side, dist, part).wait_send()


def local(
    video, gain_conv, conv_weight, gain_space, query_weight, key_weight, value_weight, out_weight,
    gain_time, time_query, time_key, time_value, time_out,
):
    vm = pltpu.VMEM
    dma = pltpu.SemaphoreType.DMA
    decoded = pl.pallas_call(
        kernel,
        out_shape=jax.ShapeDtypeStruct((T, D), BF),
        in_specs=[pl.BlockSpec(memory_space=pl.ANY)] * 13,
        out_specs=pl.BlockSpec(memory_space=pl.ANY),
        scratch_shapes=[
            vm((T, D), BF), vm((2, W, D), BF), vm((1, D), F32), vm((1, D), F32), vm((1, D), F32),
            vm((3, 3 * D, D), BF), *[vm((D, D), BF) for _ in range(9)], vm((D, 2 * D), BF), vm((FRAMES * PIECE, D), BF), vm((FRAMES * PIECE, D), BF),
            vm((4 * W, 3 * D), BF), vm((T, D), F32), vm((T, D), BF), vm((T, D), BF), vm((T, D), BF), vm((2 * ZS * T, D), BF),
            vm((T, D), BF), vm((T, 128), F32), vm((T, 128), F32), vm((T, D), F32), vm((T, D), BF),
            vm((2, FRAMES * PIECE, D), BF), vm((2, FRAMES * PIECE, D), BF),
            dma((15,)), dma((2,)), dma((2,)), dma((5,)), dma((5,)),
            dma((2, 4, 4)), dma((2, 4, 4)), dma((2, 5, 2)), dma((2, 5, 2)),
            dma((PIECES,)), dma((2, FRAMES)), dma((2,)), dma((2, FRAMES)), dma((PIECES,)), dma((2,)), pltpu.SemaphoreType.REGULAR((3,)),
        ],
        compiler_params=pltpu.CompilerParams(
            collective_id=0, has_side_effects=True, vmem_limit_bytes=56 * 1024 * 1024
        ),
    )(
        video.reshape(T, D), gain_conv.reshape(1, D), conv_weight.reshape(3, 3 * D, D), gain_space.reshape(1, D),
        query_weight, key_weight, value_weight, out_weight, gain_time.reshape(1, D),
        time_query, time_key, time_value, time_out,
    )
    return decoded.reshape(1, 2, W, D)


def solution(mesh):
    return jax.shard_map(
        local,
        mesh=mesh,
        in_specs=(P("tm", "space", None, None),) + (P(),) * 12,
        out_specs=P("tm", "space", None, None),
        check_vma=False,
    )
```

```python
import functools
import math

import jax
import jax.numpy as jnp
from jax import lax
from jax.experimental import pallas as pl
from jax.experimental.pallas import tpu as pltpu
from jax.sharding import PartitionSpec as P

epsilon = 1e-06
MESH = pl.DeviceIdType.MESH
XS, YL, CORES, YH, ZS = 4, 2, 2, 2, 8
TM = XS * YL * CORES
FRAMES = 16
W = 160
D = 512
T = 2 * W
HALF = T // 2
PIECE = 16
PIECES = T // PIECE
SCALE = 1.0 / math.sqrt(D)
LOG2E = math.log2(math.e)
BF = jnp.bfloat16
F32 = jnp.float32

QUARTER = T // 4
KEYS = 2 * T
STEPS = ZS * 2 * T // KEYS


def channel_norm(values, gains):
    average = jnp.mean(values, axis=-1, keepdims=True)
    centered = values - average
    spread = jnp.mean(centered * centered, axis=-1, keepdims=True)
    return centered * lax.rsqrt(spread + epsilon) * gains


def dot(a, b):
    return jnp.dot(a, b, preferred_element_type=F32)


def dot_t(a, b):
    return lax.dot_general(a, b, (((1,), (1,)), ((), ())), preferred_element_type=F32)


def owner(j):
    return lax.rem(5 * j, TM)


def kernel(
    video, gain_conv, conv_w, gain_space, wq, wk, wv, wo, gain_time, tq, tk, tv, to,
    out,
    vid, halo, gc, gs, gt, cw, wq_v, wk_v, wv_v, wo_v, tq_v, tk_v, tv_v, to_v, wvo, tw, tn, tv_n,
    act3, conv_acc, ac_mine, ac_t, n_out, nall, q_v, m_v, l_v, acc_v, as_t, tbuf, dbuf,
    load_sem, halo_send, halo_recv, swap_send, swap_recv,
    ring_send, ring_recv, sib_send, sib_recv,
    a_send, a_recv, a_self, d_send, d_recv, d_self, plane_sem,
):
    tm = lax.axis_index("tm")
    sp = lax.axis_index("space")
    c = lax.rem(tm, 2)
    col = tm // 2
    h = sp // ZS
    z = lax.rem(sp, ZS)
    zp = lax.rem(z + 1, ZS)
    zm = lax.rem(z + ZS - 1, ZS)
    sibling = (col * 2 + 1 - c, sp)
    z_ids = ((tm, h * ZS + zp), (tm, h * ZS + zm))
    stays = c == h
    away = jnp.logical_not(stays)
    work = (col * 2 + h, c * ZS + z)

    barrier = pltpu.get_barrier_semaphore()
    flips = [(tm + 2 * bit - 4 * bit * lax.rem(col // bit, 2), sp) for bit in (1, 2, 4)]
    across = (tm, (1 - h) * ZS + z)
    near = [*z_ids, sibling, across, (sibling[0], across[1]), *flips]
    for other in near:
        pl.semaphore_signal(barrier, inc=1, device_id=other, device_id_type=MESH)
    crosses = jnp.logical_or(sp == ZS - 1, sp == ZS)

    @pl.when(crosses)
    def _():
        other = (tm, 2 * ZS - 1 - sp)
        pl.semaphore_signal(barrier, inc=1, device_id=other, device_id_type=MESH)

    loads = []
    for i, (src, dst) in enumerate(
        [
            (video, vid), (gain_conv, gc), (conv_w.at[1], cw.at[1]), (conv_w.at[0], cw.at[0]),
            (conv_w.at[2], cw.at[2]), (gain_space, gs), (wq, wq_v), (wk, wk_v), (wv, wv_v), (wo, wo_v),
            (gain_time, gt), (tq, tq_v), (tk, tk_v), (tv, tv_v), (to, to_v),
        ]
    ):
        loads.append(pltpu.make_async_copy(src, dst, load_sem.at[i]))
    for load in loads[:6]:
        load.start()

    pl.semaphore_wait(barrier, len(near) + jnp.where(crosses, 1, 0))

    def hear(k):
        if k:
            pl.semaphore_wait(plane_sem.at[k - 1], 1)
        if k < len(flips):
            pl.semaphore_signal(plane_sem.at[k], inc=1, device_id=flips[k], device_id_type=MESH)

    hear(0)

    has_up = sp > 0
    has_down = sp < YH * ZS - 1
    to_down = pltpu.make_async_remote_copy(
        src_ref=video.at[pl.ds(W, W)], dst_ref=halo.at[0], send_sem=halo_send.at[0], recv_sem=halo_recv.at[0],
        device_id=(tm, jnp.minimum(sp + 1, YH * ZS - 1)), device_id_type=MESH,
    )
    to_up = pltpu.make_async_remote_copy(
        src_ref=video.at[pl.ds(0, W)], dst_ref=halo.at[1], send_sem=halo_send.at[1], recv_sem=halo_recv.at[1],
        device_id=(tm, jnp.maximum(sp - 1, 0)), device_id_type=MESH,
    )

    @pl.when(has_down)
    def _():
        to_down.start()

    @pl.when(has_up)
    def _():
        to_up.start()

    for load in loads[6:]:
        load.start()
    loads[0].wait()
    loads[1].wait()
    col_index = lax.broadcasted_iota(jnp.int32, (W, D), 0)

    def activate(row, raw):
        u = channel_norm(raw.astype(F32), gc[...])
        u = (u / (1.0 + jnp.exp(-u))).astype(BF).astype(F32)
        left = jnp.where(col_index == 0, 0.0, pltpu.roll(u, 1, 0))
        right = jnp.where(col_index == W - 1, 0.0, pltpu.roll(u, W - 1, 0))
        act3[pl.ds(row * W, W), 0:D] = left.astype(BF)
        act3[pl.ds(row * W, W), D : 2 * D] = u.astype(BF)
        act3[pl.ds(row * W, W), 2 * D : 3 * D] = right.astype(BF)

    activate(1, vid[0:W])
    activate(2, vid[W:T])
    loads[2].wait()
    conv_acc[...] = vid[...].astype(F32) + dot(act3[W : 3 * W], cw[1])
    loads[3].wait()
    conv_acc[W:T] += dot(act3[W : 2 * W], cw[0])
    loads[4].wait()
    conv_acc[0:W] += dot(act3[2 * W : 3 * W], cw[2])

    my_ring = jnp.where(stays, 0, 1)

    def place_of(ring, side, dist):
        if dist == 0:
            return ring * T
        if dist == ZS // 2:
            return (4 * dist - 2 + ring) * T
        return (4 * dist - 2 + 2 * ring + side) * T

    def rows_of(ring, side, dist, start, size):
        return nall.at[pl.ds(pl.multiple_of(place_of(ring, side, dist) + start, PIECE), size)]

    def ring_piece(side, dist, part):
        return pltpu.make_async_remote_copy(
            src_ref=rows_of(my_ring, side, dist, part * QUARTER, QUARTER),
            dst_ref=rows_of(my_ring, side, dist + 1, part * QUARTER, QUARTER),
            send_sem=ring_send.at[side, dist, part], recv_sem=ring_recv.at[side, dist, part],
            device_id=z_ids[side], device_id_type=MESH,
        )

    def swap_piece(part):
        return pltpu.make_async_remote_copy(
            src_ref=n_out.at[pl.ds(part * QUARTER, QUARTER)], dst_ref=rows_of(1, 0, 0, part * QUARTER, QUARTER),
            send_sem=swap_send.at[part], recv_sem=swap_recv.at[part], device_id=work, device_id_type=MESH,
        )

    swap_conv = pltpu.make_async_remote_copy(
        src_ref=ac_mine, dst_ref=ac_t, send_sem=swap_send.at[4], recv_sem=swap_recv.at[4],
        device_id=work, device_id_type=MESH,
    )

    def sib_piece(ring, side, dist, half):
        ref = rows_of(ring, side, dist, half * HALF, HALF)
        return pltpu.make_async_remote_copy(
            src_ref=ref, dst_ref=ref, send_sem=sib_send.at[side, dist, half], recv_sem=sib_recv.at[side, dist, half],
            device_id=sibling, device_id_type=MESH,
        )

    parts = ((0, 1, 2, 3), (2, 3, 0, 1))

    def travels(side, dist, part):
        return dist < ZS // 2 - 1 or (dist == ZS // 2 - 1 and part // 2 == side)

    def halves(side, dist):
        if dist == 0:
            return (0, 1) if side == 0 else ()
        return (side, 1 - side) if dist < ZS // 2 else (side,)

    def finish_row(row, arrives, copy, tap):
        part = slice(row * W, (row + 1) * W)

        @pl.when(arrives)
        def _():
            copy.wait_recv()
            activate(3 * row, halo[row])
            conv_acc[part] += dot(act3[3 * row * W : (3 * row + 1) * W], cw[tap])

        after_conv = conv_acc[part].astype(BF)
        normed = channel_norm(after_conv.astype(F32), gs[...]).astype(BF)

        @pl.when(stays)
        def _():
            ac_t[part] = after_conv
            nall[part] = normed
            for quarter in (2 * row, 2 * row + 1):
                for side in range(2):
                    ring_piece(side, 0, quarter).start()
            sib_piece(0, 0, 0, row).start()

        @pl.when(away)
        def _():
            ac_mine[part] = after_conv
            n_out[part] = normed
            for quarter in (2 * row, 2 * row + 1):
                swap_piece(quarter).start()

    loads[5].wait()
    finish_row(0, has_up, to_down, 0)
    finish_row(1, has_down, to_up, 2)

    hear(1)

    for i in range(6, 15):
        loads[i].wait()
    wvo[...] = dot(wv_v[...], wo_v[...]).astype(BF)
    tw[:, 0:D] = (dot_t(tq_v[...], tk_v[...]) * (SCALE * LOG2E)).astype(BF)
    tw[:, D : 2 * D] = dot(tv_v[...], to_v[...]).astype(BF)

    @pl.when(away)
    def _():
        for part in range(4):
            swap_piece(part).wait_recv()
            for side in range(2):
                ring_piece(side, 0, part).start()
            if part % 2 == 1:
                sib_piece(1, 0, 0, part // 2).start()

    query = dot(nall[pl.ds(pl.multiple_of(my_ring * T, T), T)], wq_v[...]).astype(BF)
    q_v[...] = (dot_t(query, wk_v[...]) * (SCALE * LOG2E)).astype(BF)
    m_v[...] = jnp.full(m_v.shape, -1e30, F32)
    l_v[...] = jnp.zeros(l_v.shape, F32)
    acc_v[...] = jnp.zeros(acc_v.shape, F32)

    def own(dist, half):
        if dist == ZS // 2 and half == 1:
            return
        for i in (2 * half, 2 * half + 1):
            for side in range(2):
                part = parts[side][i]
                ring_piece(side, dist - 1, part).wait_recv()
                if travels(side, dist, part):
                    ring_piece(side, dist, part).start()
        for side in range(2):
            sib_piece(my_ring, side, dist, halves(side, dist)[half]).start()

    def other(dist):
        for side in range(2):
            for half in halves(side, dist):
                sib_piece(1 - my_ring, side, dist, half).wait_recv()

    order_0 = (1, 0, 3, 2, 5, 4, 6, 7)
    order_1 = (0, 1, 2, 3, 4, 5, 6, 7)
    before_0 = (
        lambda: (own(1, 0), own(1, 1)),
        lambda: (own(2, 0), other(0)),
        lambda: own(2, 1),
        lambda: (own(3, 0), other(1)),
        lambda: own(3, 1),
        lambda: (own(4, 0), other(2)),
        lambda: other(3),
        lambda: other(4),
    )
    before_1 = (
        lambda: other(0),
        lambda: other(1),
        lambda: (own(1, 0), own(1, 1), swap_conv.start()),
        lambda: (own(2, 0), other(2)),
        lambda: own(2, 1),
        lambda: (own(3, 0), other(3)),
        lambda: own(3, 1),
        lambda: (own(4, 0), other(4)),
    )

    def arrive(k):
        @pl.when(stays)
        def _():
            before_0[k]()

        @pl.when(away)
        def _():
            before_1[k]()

    def attend(t, carry):
        index = jnp.int32(0)
        for k in range(STEPS - 1):
            pl.when(t == k)(functools.partial(arrive, k))
            index = jnp.where(t == k, jnp.where(stays, order_0[k], order_1[k]), index)
        attend_rows(slice(0, T), nall[pl.ds(pl.multiple_of(index * KEYS, KEYS), KEYS)])
        return carry

    def attend_rows(rows, keys):
        s = dot_t(q_v[rows], keys)
        m_old = m_v[rows, 0:1]
        m_new = jnp.maximum(m_old, jnp.max(s, axis=1, keepdims=True))
        p = jnp.exp2(s - m_new)
        alpha = jnp.exp2(m_old - m_new)
        l_new = l_v[rows, 0:1] * alpha + jnp.sum(p, axis=1, keepdims=True)
        l_v[rows] = jnp.broadcast_to(l_new, (l_new.shape[0], 128))
        m_v[rows] = jnp.broadcast_to(m_new, (l_new.shape[0], 128))
        acc_v[rows] = acc_v[rows] * alpha + dot(p.astype(BF), keys)

    hear(2)
    lax.fori_loop(0, STEPS - 1, attend, 0)
    hear(3)

    frame = col * 2 + h
    home = c * ZS + z

    def a_piece(j, f):
        slot = j // TM
        return pltpu.make_async_remote_copy(
            src_ref=as_t.at[pl.ds(pl.multiple_of(j * PIECE, PIECE), PIECE)],
            dst_ref=tbuf.at[slot, pl.ds(pl.multiple_of(f * PIECE, PIECE), PIECE)],
            send_sem=a_send.at[j], recv_sem=a_recv.at[slot, f],
            device_id=(owner(j), home), device_id_type=MESH,
        )

    def a_local(j):
        slot = j // TM
        return pltpu.make_async_copy(
            as_t.at[pl.ds(pl.multiple_of(j * PIECE, PIECE), PIECE)],
            tbuf.at[slot, pl.ds(pl.multiple_of(frame * PIECE, PIECE), PIECE)],
            a_self.at[slot],
        )

    def is_me(j):
        return jnp.logical_and(stays, owner(j) == tm)

    def a_start(j, carry):
        @pl.when(is_me(j))
        def _():
            a_local(j).start()

        @pl.when(jnp.logical_not(is_me(j)))
        def _():
            a_piece(j, frame).start()

        return carry

    arrive(STEPS - 1)

    @pl.when(away)
    def _():
        swap_conv.wait_recv()

    for start, stop in ((0, 6), (6, PIECES)):
        part = slice(start * PIECE, stop * PIECE)
        attend_rows(part, nall[(STEPS - 1) * KEYS :])
        mixed = (acc_v[part] / l_v[part, 0:1]).astype(BF)
        as_t[part] = (ac_t[part].astype(F32) + dot(mixed, wvo[...])).astype(BF)
        lax.fori_loop(start, stop, a_start, 0, unroll=True)

    first = lax.rem(13 * tm, TM)
    has_second = first < PIECES - TM

    rows = FRAMES * PIECE
    r_index = lax.broadcasted_iota(jnp.int32, (rows, rows), 0)
    c_index = lax.broadcasted_iota(jnp.int32, (rows, rows), 1)
    allowed = jnp.logical_and((r_index & (PIECE - 1)) == (c_index & (PIECE - 1)), r_index >= c_index)

    def d_piece(slot, j, f):
        return pltpu.make_async_remote_copy(
            src_ref=dbuf.at[slot, pl.ds(pl.multiple_of(f * PIECE, PIECE), PIECE)],
            dst_ref=out.at[pl.ds(pl.multiple_of(j * PIECE, PIECE), PIECE)],
            send_sem=d_send.at[slot, f], recv_sem=d_recv.at[j],
            device_id=(f, sp), device_id_type=MESH,
        )

    def d_local(slot, j):
        return pltpu.make_async_copy(
            dbuf.at[slot, pl.ds(pl.multiple_of(tm * PIECE, PIECE), PIECE)],
            out.at[pl.ds(pl.multiple_of(j * PIECE, PIECE), PIECE)],
            d_self.at[slot],
        )

    def temporal(slot, j):
        def wait_piece(f, carry):
            own = jnp.logical_and(stays, f == frame)

            @pl.when(own)
            def _():
                a_local(j).wait()

            @pl.when(jnp.logical_not(own))
            def _():
                a_piece(slot * TM, f).wait_recv()

            return carry

        def d_start(f, carry):
            @pl.when(f == tm)
            def _():
                d_local(slot, j).start()

            @pl.when(f != tm)
            def _():
                d_piece(slot, j, f).start()

            return carry

        middle = rows // 2
        for begin, end in ((0, middle), (middle, rows)):
            lax.fori_loop(begin // PIECE, end // PIECE, wait_piece, 0)
            x = tbuf[slot, begin:end]
            normed = channel_norm(x.astype(F32), gt[...]).astype(BF)
            qv = dot(normed, tw[...]).astype(BF)
            tn[begin:end] = normed
            tv_n[begin:end] = qv[:, D:]
            s = jnp.where(allowed[begin:end, 0:end], dot_t(qv[:, 0:D], tn[0:end]), -1e30)
            p = jnp.exp2(s - jnp.max(s, axis=1, keepdims=True))
            total = jnp.sum(p, axis=1, keepdims=True)
            dbuf[slot, begin:end] = (x.astype(F32) + dot(p.astype(BF), tv_n[0:end]) / total).astype(BF)
            lax.fori_loop(begin // PIECE, end // PIECE, d_start, 0, unroll=True)

    temporal(0, first)

    @pl.when(has_second)
    def _():
        temporal(1, TM + first)

    def d_wait(j, carry):
        mine = owner(j) == tm

        @pl.when(mine)
        def _():
            d_local(j // TM, j).wait()

        @pl.when(jnp.logical_not(mine))
        def _():
            d_piece(0, j, tm).wait_recv()

        return carry

    lax.fori_loop(0, PIECES, d_wait, 0)

    def a_sent(j, carry):
        @pl.when(jnp.logical_not(is_me(j)))
        def _():
            a_piece(j, frame).wait_send()

        return carry

    lax.fori_loop(0, PIECES, a_sent, 0)

    def d_sent(f, carry):
        @pl.when(f != tm)
        def _():
            d_piece(0, tm, f).wait_send()

            @pl.when(has_second)
            def _():
                d_piece(1, tm, f).wait_send()

        return carry

    lax.fori_loop(0, FRAMES, d_sent, 0)

    @pl.when(has_down)
    def _():
        to_down.wait_send()

    @pl.when(has_up)
    def _():
        to_up.wait_send()

    @pl.when(away)
    def _():
        swap_conv.wait_send()
        for part in range(4):
            swap_piece(part).wait_send()

    for dist in range(ZS // 2 + 1):
        for side in range(2):
            for half in halves(side, dist):
                sib_piece(my_ring, side, dist, half).wait_send()
            for part in parts[side]:
                if travels(side, dist, part):
                    ring_piece(side, dist, part).wait_send()


def local(
    video, gain_conv, conv_weight, gain_space, query_weight, key_weight, value_weight, out_weight,
    gain_time, time_query, time_key, time_value, time_out,
):
    vm = pltpu.VMEM
    dma = pltpu.SemaphoreType.DMA
    decoded = pl.pallas_call(
        kernel,
        out_shape=jax.ShapeDtypeStruct((T, D), BF),
        in_specs=[pl.BlockSpec(memory_space=pl.ANY)] * 13,
        out_specs=pl.BlockSpec(memory_space=pl.ANY),
        scratch_shapes=[
            vm((T, D), BF), vm((2, W, D), BF), vm((1, D), F32), vm((1, D), F32), vm((1, D), F32),
            vm((3, 3 * D, D), BF), *[vm((D, D), BF) for _ in range(9)], vm((D, 2 * D), BF), vm((FRAMES * PIECE, D), BF), vm((FRAMES * PIECE, D), BF),
            vm((4 * W, 3 * D), BF), vm((T, D), F32), vm((T, D), BF), vm((T, D), BF), vm((T, D), BF), vm((2 * ZS * T, D), BF),
            vm((T, D), BF), vm((T, 128), F32), vm((T, 128), F32), vm((T, D), F32), vm((T, D), BF),
            vm((2, FRAMES * PIECE, D), BF), vm((2, FRAMES * PIECE, D), BF),
            dma((15,)), dma((2,)), dma((2,)), dma((5,)), dma((5,)),
            dma((2, 4, 4)), dma((2, 4, 4)), dma((2, 5, 2)), dma((2, 5, 2)),
            dma((PIECES,)), dma((2, FRAMES)), dma((2,)), dma((2, FRAMES)), dma((PIECES,)), dma((2,)), pltpu.SemaphoreType.REGULAR((3,)),
        ],
        compiler_params=pltpu.CompilerParams(
            collective_id=0, has_side_effects=True, vmem_limit_bytes=56 * 1024 * 1024
        ),
    )(
        video.reshape(T, D), gain_conv.reshape(1, D), conv_weight.reshape(3, 3 * D, D), gain_space.reshape(1, D),
        query_weight, key_weight, value_weight, out_weight, gain_time.reshape(1, D),
        time_query, time_key, time_value, time_out,
    )
    return decoded.reshape(1, 2, W, D)


def solution(mesh):
    return jax.shard_map(
        local,
        mesh=mesh,
        in_specs=(P("tm", "space", None, None),) + (P(),) * 12,
        out_specs=P("tm", "space", None, None),
        check_vma=False,
    )
```
